256 devices in a mesh: img: 16 (over x_lo, y, core), patch: 16 (over z, x_hi).
Axes of the slice: x: 4 (x_hi: 2, x_lo: 2; x = x_hi * 2 + x_lo), y: 4, z: 8, core: 2. Of those that a mesh axis runs over, the one named last changes fastest.
Arguments:
- latents: bfloat16 [16384, 1280], P(('img', 'patch')), parts along dimension 0, may hold values from -108 to 108
- timestep: int32 [16], P('img'), parts along dimension 0, may hold values from 0 to 999
- gn_gain: float32 [1280], replicated, may hold values from 0.1 to 1.9
- gn_shift: float32 [1280], replicated, may hold values from -3 to 3
- temb_weight: bfloat16 [320, 1280], replicated, may hold values from -0.3125 to 0.3125
- w_query: bfloat16 [1280, 1280], P('patch'), may hold values from -0.4375 to 0.4375
- w_keyval: bfloat16 [1280, 2560], P('patch'), may hold values from -0.15625 to 0.15625
- w_out: bfloat16 [1280, 1280], P('patch'), may hold values from -0.15625 to 0.15625
- stale_kv: bfloat16 [2, 16384, 1280], P(None, ('img', 'patch')), parts along dimension 1, may hold values from -96 to 96
Outputs:
- mixed: bfloat16 [16384, 1280], P(('img', 'patch')), parts along dimension 0
The draws below stay inside these ranges and needn't reach their ends.
There are 16 independent parts, one for each index of `img`. The reference program is written for one: setup_inputs(seed, part) draws one part's arguments, and reference() takes and returns one part's arrays. A program takes and returns all parts, laid end to end along the dimension named above; an argument that names none is the same for every part. Nothing has to cross between parts.
All inputs are finite; a program needn't handle non-finite values.
Results may differ from the reference program's by a relative error of at most 0.0064.
The reference program's roundings to bfloat16 on the way (of `embed`, `normed`, `probs` and `attended`) count: a program that leaves them out, or rounds other values in their place, can miss the bound.
Values may be sent and summed in bfloat16 or wider, within the bound.
A program may use at most 64 MiB of HBM per device.

```python
import math
import jax
import jax.numpy as jnp
from jax import lax

D = 1280
TEMB = 320
HEAD_DIM = 64
GROUPS = 32
TOK_DEV = 64
HEADS = 20
TOKENS = 1024
N_PATCH = 16


def draw_latents(key, part):
    key = jax.random.fold_in(key, 11)
    first, second, third = jax.random.split(key, 3)
    position = jnp.arange(TOKENS, dtype=jnp.float32) / max(TOKENS - 1, 1)
    rise = (1.0 + 2.0 * position)[:, None]
    base = jnp.clip(jax.random.normal(first, (TOKENS, D), jnp.float32), -4.0, 4.0)
    rough = jnp.exp(jax.random.uniform(second, (TOKENS, 1), jnp.float32) * math.log(10.0)) * 0.3
    column = jnp.exp(jax.random.uniform(third, (1, D), jnp.float32) * math.log(10.0)) * 0.3
    return (base * rise * rough * column).astype(jnp.bfloat16)


def draw_stale_kv(key, part):
    key = jax.random.fold_in(key, 23)
    first = jax.random.fold_in(key, 0)
    base = jnp.clip(jax.random.normal(first, (2, TOKENS, D), jnp.float32), -4.0, 4.0)
    return base.astype(jnp.bfloat16)


def shard_levels(rng, dims, pieces, low, high):
    def one(dim, shards_of):
        draws = jax.random.uniform(jax.random.fold_in(jax.random.fold_in(rng, 6), dim), (shards_of,), jnp.float32, low / len(pieces), high / len(pieces))
        return jnp.repeat(jnp.exp(draws), dims[dim] // shards_of).reshape((-1,) + (1,) * (len(dims) - dim - 1))

    level = one(*pieces[0])
    for cut in pieces[1:]:
        level = level * one(*cut)
    return level


def gaussian(rng, shape, width, bound, pieces=(), held_as=jnp.bfloat16):
    gain = shard_levels(rng, shape, pieces, -0.22, 0.18) if pieces else 1.0
    drawn = jax.random.normal(rng, shape, jnp.float32) * width * gain
    return jnp.minimum(jnp.maximum(drawn, -bound), bound).astype(held_as)


def setup_inputs(seed: int = 0, part: int = 0) -> dict:
    seeds = jax.random.split(jax.random.key(seed), 10)
    part_splits = jax.random.split(jax.random.fold_in(seeds[9], part), 10)
    latents = draw_latents(jax.random.fold_in(jax.random.fold_in(seeds[9], part), 71), part)
    timestep = jax.random.randint(part_splits[1], (1,), 0, 1000).astype(jnp.int32)
    gn_gain = jnp.clip(1.0 + 0.18 * jax.random.normal(seeds[2], (D,), jnp.float32), 0.1, 1.9)
    gn_shift = gaussian(seeds[3], (D,), 0.5, 3.0, (), jnp.float32)
    temb_weight = gaussian(seeds[4], (TEMB, D), TEMB ** -0.5, 0.3125)
    w_query = gaussian(seeds[5], (D, D), (D // 6) ** -0.5, 0.4375, ((0, 16),))
    w_keyval = gaussian(seeds[6], (D, 2 * D), D ** -0.5, 0.15625, ((0, 16),))
    w_out = gaussian(seeds[7], (D, D), D ** -0.5, 0.15625, ((0, 16),))
    stale_kv = draw_stale_kv(jax.random.fold_in(jax.random.fold_in(seeds[9], part), 71), part)
    return dict(latents=latents, timestep=timestep, gn_gain=gn_gain, gn_shift=gn_shift, temb_weight=temb_weight, w_query=w_query, w_keyval=w_keyval, w_out=w_out, stale_kv=stale_kv)


EPS = 1e-06

def time_shift(timestep, temb_weight):
    half = temb_weight.shape[0] // 2
    freqs = jnp.exp(-math.log(10000.0) * jnp.arange(half, dtype=jnp.float32) / half)
    angles = timestep.astype(jnp.float32)[0] * freqs
    embed = jnp.concatenate([jnp.cos(angles), jnp.sin(angles)]).astype(jnp.bfloat16)
    return jax.nn.silu(jnp.dot(embed[None, :], temb_weight, preferred_element_type=jnp.float32))

def reference(latents, timestep, gn_gain, gn_shift, temb_weight, w_query, w_keyval, w_out, stale_kv):
    hidden = latents.astype(jnp.float32) + time_shift(timestep, temb_weight)
    grouped = hidden.reshape(TOKENS, GROUPS, D // GROUPS)
    count = TOKENS * (D // GROUPS)
    mean = lax.optimization_barrier(jnp.sum(grouped, axis=(0, 2))) / count
    centered = grouped - mean[None, :, None]
    var = lax.optimization_barrier(jnp.sum(centered * centered, axis=(0, 2))) / count
    scaled = (centered * lax.rsqrt(var + EPS)[None, :, None]).reshape(TOKENS, D)
    normed = (scaled * gn_gain + gn_shift).astype(jnp.bfloat16)
    query = jnp.dot(normed, w_query, preferred_element_type=jnp.float32).astype(jnp.bfloat16)
    keyval = jnp.dot(normed, w_keyval, preferred_element_type=jnp.float32).astype(jnp.bfloat16)
    fresh_keys = keyval[:, :D].reshape(N_PATCH, TOK_DEV, HEADS, HEAD_DIM)
    fresh_values = keyval[:, D:].reshape(N_PATCH, TOK_DEV, HEADS, HEAD_DIM)
    stale_keys = stale_kv[0].reshape(N_PATCH, TOK_DEV, HEADS, HEAD_DIM)
    stale_values = stale_kv[1].reshape(N_PATCH, TOK_DEV, HEADS, HEAD_DIM)
    queries = query.reshape(N_PATCH, TOK_DEV, HEADS, HEAD_DIM)
    block_ids = jnp.arange(N_PATCH, dtype=jnp.int32)

    def one_block(index):
        own = (block_ids == index)[:, None, None, None]
        keys = jnp.where(own, fresh_keys[index][None], stale_keys).astype(jnp.float32)
        values = jnp.where(own, fresh_values[index][None], stale_values).astype(jnp.float32)
        local_q = queries[index].astype(jnp.float32)
        scores = jnp.einsum('qhd,jkhd->hqjk', local_q, keys) * 0.125
        top = lax.optimization_barrier(jnp.max(scores, axis=-1))
        rounded = lax.optimization_barrier(jnp.exp(scores - top[..., None]).astype(jnp.bfloat16))
        probs = rounded.astype(jnp.float32)
        numer = jnp.einsum('hqjk,jkhd->hqjd', probs, values)
        denom = lax.optimization_barrier(jnp.sum(probs, axis=-1))
        peak = lax.optimization_barrier(jnp.max(top, axis=-1))
        weight = jnp.exp(top - peak[..., None])
        total = lax.optimization_barrier(jnp.sum(weight[..., None] * numer, axis=2)) / lax.optimization_barrier(jnp.sum(weight * denom, axis=2))[..., None]
        return jnp.transpose(total, (1, 0, 2)).reshape(TOK_DEV, D).astype(jnp.bfloat16)
    attended = lax.map(one_block, block_ids).reshape(TOKENS, D)
    projected = jnp.dot(attended, w_out, preferred_element_type=jnp.float32)
    return (hidden + projected).astype(jnp.bfloat16)
```

```python
import math

import jax
import jax.numpy as jnp
from jax import lax
from jax.experimental import pallas as pl
from jax.experimental.pallas import tpu as pltpu
from jax.sharding import PartitionSpec as P

MESH = pl.DeviceIdType.MESH
BF = jnp.bfloat16
F32 = jnp.float32
D = 1280
HALF = 640
TOK = 64
NZ = 8
NY = 4
GROUPS = 32
GROUP_WIDTH = D // GROUPS
TEMB = 320
EPS = 1e-06
PHASES = ((0, 2), (2, 5))
EXP2_SCALE = 0.125 * math.log2(math.e)
NT = (((1,), (1,)), ((), ()))
TN = (((0,), (0,)), ((), ()))


def split3(x):
    high = x.astype(BF)
    rest = x - high.astype(F32)
    mid = rest.astype(BF)
    low = (rest - mid.astype(F32)).astype(BF)
    return [high, mid, low]


def stack_rows(rows, width):
    index = lax.broadcasted_iota(jnp.int32, (16, width), 0)
    out = jnp.zeros((16, width), F32)
    for k, row in enumerate(rows):
        out = jnp.where(index == k, jnp.broadcast_to(row.astype(F32), (16, width)), out)
    return out.astype(BF)


def kernel(
    ts_ref, lat_ref, gain_ref, shift_ref, temb_ref, wq_ref, wkv_ref, wo_ref, stale_ref,
    out_ref,
    wst, wbuf, kvbuf, latb, hid, normed, grp, stown, stb, q2, kfr, vfr, top_s, den_s, acc_s,
    att, mixs, mixr,
    ld_sem, wx_send, wx_recv, wz_send, wz_recv, wy_send, wy_recv, wc_send, wc_recv,
    lat_send, lat_recv, sx_send, sx_recv, sz_send, sz_recv, own_sem,
    st_send, st_recv, at_send, at_recv, mx_send, mx_recv,
):
    img = lax.axis_index("img")
    patch = lax.axis_index("patch")
    xl, y, c = img // 8, (img // 2) % 4, img % 2
    z, h = patch // 2, patch % 2
    sgn = 1 - 2 * c

    def at_dev(xl_, y_, c_, z_, h_):
        return {"img": xl_ * 8 + y_ * 2 + c_, "patch": z_ * 2 + h_}

    def zmod(k):
        return (z + k + 2 * NZ) % NZ

    def ymod(k):
        return (y + k + 2 * NY) % NY

    d_zp, d_zm = at_dev(xl, y, c, zmod(sgn), h), at_dev(xl, y, c, zmod(-sgn), h)
    d_yp, d_ym = at_dev(xl, ymod(sgn), c, z, h), at_dev(xl, ymod(-sgn), c, z, h)
    d_c = at_dev(xl, y, 1 - c, z, h)
    d_x = at_dev(xl, y, c, z, 1 - h)
    d_n = at_dev(1 - xl, y, c, z, 1 - h)
    z_peers = [at_dev(xl, y, c, zmod(k), h) for k in range(1, NZ)]

    sends = []

    def remote(src, dst, ssem, rsem, dev):
        return pltpu.make_async_remote_copy(
            src_ref=src, dst_ref=dst, send_sem=ssem, recv_sem=rsem, device_id=dev, device_id_type=MESH
        )

    def send(src, dst, ssem, rsem, dev):
        copy = remote(src, dst, ssem, rsem, dev)
        copy.start()
        sends.append(copy)

    def arrived(dst, ssem, rsem, dev):
        remote(dst, dst, ssem, rsem, dev).wait_recv()

    loads = [
        pltpu.make_async_copy(wq_ref, wst.at[:, 0:D], ld_sem.at[0]),
        pltpu.make_async_copy(wkv_ref, wst.at[:, D:3 * D], ld_sem.at[1]),
        pltpu.make_async_copy(wo_ref, wst.at[:, 3 * D:4 * D], ld_sem.at[2]),
    ]
    for copy in loads:
        copy.start()
    barrier = pltpu.get_barrier_semaphore()
    greeted = z_peers + [d_yp, d_ym, d_c, d_x, d_n]
    for dev in greeted:
        pl.semaphore_signal(barrier, inc=1, device_id=dev, device_id_type=MESH)
    my_cols = pl.ds(pl.multiple_of(HALF * h, 128), HALF)
    other_cols = pl.ds(pl.multiple_of(HALF * (1 - h), 128), HALF)
    own_kv = pltpu.make_async_copy(stale_ref.at[:, :, my_cols], kvbuf.at[z, h], own_sem)
    own_kv.start()

    lane = lax.broadcasted_iota(jnp.int32, (1, TEMB), 1)
    half = TEMB // 2
    k = jnp.where(lane < half, lane, lane - half).astype(F32)
    freqs = jnp.exp(-math.log(10000.0) * k / half)
    angles = ts_ref[0].astype(F32) * freqs
    embed = jnp.where(lane < half, jnp.cos(angles), jnp.sin(angles)).astype(BF)
    embed = stack_rows([embed], TEMB)
    pre = jnp.dot(embed, temb_ref[...], preferred_element_type=F32)[0:1]
    shift_vec = pre * (1.0 / (1.0 + jnp.exp(-pre)))
    channel = lax.broadcasted_iota(jnp.int32, (D, 128), 0)
    first = lax.broadcasted_iota(jnp.int32, (D, 128), 1) * GROUP_WIDTH
    grp[...] = jnp.where((channel >= first) & (channel < first + GROUP_WIDTH), 1.0, 0.0).astype(BF)
    latb[h] = lat_ref[...]

    for copy in loads:
        copy.wait()
    pl.semaphore_wait(barrier, len(greeted))

    def rows_of(zz, cc):
        return pl.ds(pl.multiple_of(160 * zz + 80 * cc, 16), 80)

    def tile_cols(j, hh):
        t = 4 * j + y
        return pl.ds(pl.multiple_of(D * (t // 5) + HALF * hh + 128 * (t % 5), 128), 128)

    @pl.when(c == h)
    def _():
        for ph, (j0, j1) in enumerate(PHASES):
            for j in range(j0, j1):
                remote(
                    wst.at[:, tile_cols(j, 1 - h)], wbuf.at[j, y, rows_of(z, c)],
                    wx_send.at[j], wx_recv.at[ph], d_n,
                ).start()
        for ph, (j0, j1) in enumerate(PHASES):
            for j in range(j0, j1):
                pltpu.make_async_copy(
                    wst.at[:, tile_cols(j, h)], wbuf.at[j, y, rows_of(z, c)], wx_recv.at[ph]
                ).start()

    send(lat_ref, latb.at[h], lat_send, lat_recv, d_x)
    send(stale_ref.at[:, :, other_cols], kvbuf.at[z, h], sx_send, sx_recv, d_x)

    def unit(ph, yy, zz):
        j0, j1 = PHASES[ph]
        return wbuf.at[j0:j1, yy, rows_of(zz, c)]

    def zslot(m):
        return zmod(-sgn * m) if m <= 4 else zmod(sgn * (m - 4))

    def slots(tick):
        return [m for m in (tick, tick + 4 if 1 <= tick <= 3 else None) if m is not None]

    def w_stage(ph, tick):
        for m in slots(tick):
            zz = zslot(m)
            ref = unit(ph, y, zz)
            if m == 0:
                pltpu.make_async_copy(ref, ref, wx_recv.at[ph]).wait()
            else:
                arrived(ref, wz_send.at[ph, m - 1], wz_recv.at[ph, m - 1], d_zp)
            if m <= 3:
                send(ref, ref, wz_send.at[ph, m], wz_recv.at[ph, m], d_zp)
            if m == 0 or 5 <= m <= 6:
                nxt = 4 if m == 0 else m
                send(ref, ref, wz_send.at[ph, nxt], wz_recv.at[ph, nxt], d_zm)
            send(ref, ref, wy_send.at[ph, m, 0], wy_recv.at[ph, m, 0], d_yp)
            send(ref, ref, wy_send.at[ph, m, 1], wy_recv.at[ph, m, 1], d_ym)

    def y_stage(ph, tick):
        for m in slots(tick):
            zz = zslot(m)
            ref = unit(ph, ymod(-sgn), zz)
            arrived(ref, wy_send.at[ph, m, 0], wy_recv.at[ph, m, 0], d_yp)
            send(ref, ref, wy_send.at[ph, m, 2], wy_recv.at[ph, m, 2], d_yp)

    def c_stage(ph, tick):
        j0, j1 = PHASES[ph]
        for m in slots(tick):
            zz = zslot(m)
            arrived(unit(ph, ymod(sgn), zz), wy_send.at[ph, m, 1], wy_recv.at[ph, m, 1], d_ym)
            arrived(unit(ph, ymod(2), zz), wy_send.at[ph, m, 2], wy_recv.at[ph, m, 2], d_yp)
            ref = wbuf.at[j0:j1, :, rows_of(zz, c)]
            send(ref, ref, wc_send.at[ph, m], wc_recv.at[ph, m], d_c)

    def w_ready(ph):
        j0, j1 = PHASES[ph]
        for m in range(8):
            zz = zmod(sgn * m) if m <= 4 else zmod(-sgn * (m - 4))
            arrived(wbuf.at[j0:j1, :, rows_of(zz, 1 - c)], wc_send.at[ph, m], wc_recv.at[ph, m], d_c)

    def s_stage(tick):
        for m in slots(tick):
            zz = zslot(m)
            for part in range(2):
                ref = kvbuf.at[zz, h if part == 0 else 1 - h]
                src = ref
                if m == 0:
                    if part == 0:
                        src = stale_ref.at[:, :, my_cols]
                    else:
                        arrived(ref, sx_send, sx_recv, d_x)
                else:
                    arrived(ref, sz_send.at[m - 1, part], sz_recv.at[m - 1, part], d_zp)
                if m <= 3:
                    send(src, ref, sz_send.at[m, part], sz_recv.at[m, part], d_zp)
                if m == 0 or 5 <= m <= 6:
                    nxt = 4 if m == 0 else m
                    send(src, ref, sz_send.at[nxt, part], sz_recv.at[nxt, part], d_zm)

    def group_sums(x):
        sums = jnp.dot(stack_rows(split3(x), D), grp[...], preferred_element_type=F32)
        return jnp.sum(sums, axis=0, keepdims=True)

    def to_channels(values):
        rows = []
        for v in values:
            rows += split3(v)
        spread = lax.dot_general(stack_rows(rows, 128), grp[...], NT, preferred_element_type=F32)
        return [jnp.sum(spread[3 * i:3 * i + 3], axis=0, keepdims=True) for i in range(len(values))]

    local_count = float(2 * TOK * GROUP_WIDTH)

    def stats_send():
        arrived(latb.at[1 - h], lat_send, lat_recv, d_x)
        for xh in range(2):
            hid[TOK * xh:TOK * xh + TOK] = latb[xh].astype(F32) + shift_vec
        sums = group_sums(jnp.sum(hid[...], axis=0, keepdims=True))
        (local_mean,) = to_channels([sums / local_count])
        centered = hid[...] - local_mean
        squares = group_sums(jnp.sum(centered * centered, axis=0, keepdims=True))
        stown[0:1] = sums
        stown[1:2] = squares
        for n in range(1, NZ):
            send(stown, stb.at[n - 1], st_send.at[n - 1], st_recv.at[n - 1], z_peers[n - 1])

    def normalise():
        for n in range(1, NZ):
            arrived(stb.at[n - 1], st_send.at[n - 1], st_recv.at[n - 1], z_peers[n - 1])
        parts = [stown[0:2]] + [stb[n, 0:2] for n in range(NZ - 1)]
        mean = sum(part[0:1] for part in parts) / (NZ * local_count)
        total = jnp.zeros_like(mean)
        for part in parts:
            away = part[0:1] / local_count - mean
            total += part[1:2] + local_count * (away * away)
        rstd = lax.rsqrt(total / (NZ * local_count) + EPS)
        mean, rstd = to_channels([mean, rstd])
        gain, shift = gain_ref[...], shift_ref[...]
        for r in range(0, 2 * TOK, 16):
            scaled = (hid[r:r + 16] - mean) * rstd
            normed[r:r + 16] = (scaled * gain + shift).astype(BF)

    def weight_tile(t):
        return wbuf[t // 4, t % 4]

    q_lane = lax.broadcasted_iota(jnp.int32, (2 * TOK, 128), 1)

    def query_projection():
        for t in range(5):
            q = jnp.dot(normed[...], weight_tile(t), preferred_element_type=F32)
            q2[t, 0:128] = jnp.where(q_lane < 64, q, 0.0).astype(BF)
            q2[t, 128:256] = jnp.where(q_lane < 64, 0.0, q).astype(BF)

    def keyval_projection():
        for t in range(5):
            kfr[t] = jnp.dot(normed[...], weight_tile(5 + t), preferred_element_type=F32).astype(BF)
            vfr[t] = jnp.dot(normed[...], weight_tile(10 + t), preferred_element_type=F32).astype(BF)

    def block(q, key, value, mask):
        s = lax.dot_general(key, q, NT, preferred_element_type=F32)
        if mask is not None:
            s = jnp.where(mask, s, -jnp.inf)
        top = jnp.max(s, axis=0, keepdims=True)
        probs = jnp.exp2((s - top) * EXP2_SCALE).astype(BF)
        denom = jnp.sum(probs.astype(F32), axis=0, keepdims=True)
        both = lax.dot_general(value, probs, TN, preferred_element_type=F32)
        numer = jnp.concatenate([both[0:64, 0:128], both[64:128, 128:256]], axis=1)
        return top, numer, denom

    def merge(t, results):
        peak = top_s[t]
        new_peak = peak
        for top, _, _ in results:
            new_peak = jnp.maximum(new_peak, top)
        keep = jnp.exp2((peak - new_peak) * EXP2_SCALE)
        numer, denom = acc_s[t] * keep, den_s[t] * keep
        for top, part_numer, part_denom in results:
            weight = jnp.exp2((top - new_peak) * EXP2_SCALE)
            numer += weight * part_numer
            denom += weight * part_denom
        top_s[t], acc_s[t], den_s[t] = new_peak, numer, denom

    def attend(zzs):
        def step(t, carry):
            cols = pl.ds(pl.multiple_of(128 * t, 128), 128)
            q = q2[t]
            merge(t, [
                block(q, kvbuf[zz, xh, 0, :, cols], kvbuf[zz, xh, 1, :, cols], None)
                for zz in zzs for xh in range(2)
            ])
            return carry

        lax.fori_loop(0, 5, step, 0)

    def attend_own():
        row = lax.broadcasted_iota(jnp.int32, (128, 256), 0)
        block_of = (lax.broadcasted_iota(jnp.int32, (128, 256), 1) // TOK) % 2

        def step(t, carry):
            cols = pl.ds(pl.multiple_of(128 * t, 128), 128)
            q = q2[t]
            results = []
            for xh in range(2):
                mask = (row < 64) == (block_of == xh)
                rows = slice(TOK * xh, TOK * xh + TOK)
                key = jnp.concatenate([kfr[t, rows], kvbuf[z, xh, 0, :, cols]], axis=0)
                value = jnp.concatenate([vfr[t, rows], kvbuf[z, xh, 1, :, cols]], axis=0)
                results.append(block(q, key, value, mask))
            merge(t, results)
            return carry

        lax.fori_loop(0, 5, step, 0)

    def finish_attention():
        for t in range(5):
            ratio = acc_s[t] / den_s[t]
            turned = jnp.concatenate([ratio[:, 0:128], ratio[:, 128:256]], axis=0).T
            cols = pl.ds(pl.multiple_of(HALF * h + 128 * t, 128), 128)
            att[:, cols] = turned.astype(BF)
            send(att.at[:, cols], att.at[:, cols], at_send.at[t], at_recv.at[t], d_x)

    def output_projection():
        for t in range(5):
            cols = pl.ds(pl.multiple_of(HALF * (1 - h) + 128 * t, 128), 128)
            arrived(att.at[:, cols], at_send.at[t], at_recv.at[t], d_x)
        for t in range(5):
            cols = pl.ds(pl.multiple_of(HALF * h + 128 * t, 128), 128)
            mixed = hid[:, cols] + jnp.dot(att[...], weight_tile(15 + t), preferred_element_type=F32)
            mixed = mixed.astype(BF)
            for xh in range(2):
                mixs[xh, :, 128 * t:128 * t + 128] = mixed[TOK * xh:TOK * xh + TOK]
        send(mixs.at[1 - h], mixr, mx_send, mx_recv, d_x)
        out_ref[:, my_cols] = mixs[h]
        arrived(mixr, mx_send, mx_recv, d_x)
        out_ref[:, other_cols] = mixr[...]

    top_s[...] = jnp.full(top_s.shape, -jnp.inf, F32)
    den_s[...] = jnp.zeros(den_s.shape, F32)
    acc_s[...] = jnp.zeros(acc_s.shape, F32)

    w_stage(0, 0)
    s_stage(0)
    stats_send()
    w_stage(0, 1)
    y_stage(0, 0)
    w_stage(1, 0)
    w_stage(0, 2)
    y_stage(0, 1)
    c_stage(0, 0)
    w_stage(0, 3)
    y_stage(0, 2)
    c_stage(0, 1)
    s_stage(1)
    w_stage(0, 4)
    y_stage(0, 3)
    c_stage(0, 2)
    w_stage(1, 1)
    y_stage(0, 4)
    c_stage(0, 3)
    y_stage(1, 0)
    c_stage(0, 4)
    w_stage(1, 2)
    normalise()
    w_ready(0)
    query_projection()
    s_stage(2)
    y_stage(1, 1)
    c_stage(1, 0)
    w_stage(1, 3)
    attend([zslot(1), zslot(5)])
    y_stage(1, 2)
    c_stage(1, 1)
    w_stage(1, 4)
    y_stage(1, 3)
    c_stage(1, 2)
    s_stage(3)
    y_stage(1, 4)
    c_stage(1, 3)
    attend([zslot(2), zslot(6)])
    c_stage(1, 4)
    w_ready(1)
    keyval_projection()
    own_kv.wait()
    attend_own()
    attend([zslot(3), zslot(7)])
    s_stage(4)
    attend([zslot(4)])
    finish_attention()
    output_projection()

    for copy in sends:
        copy.wait_send()

    @pl.when(c == h)
    def _():
        for j in range(5):
            remote(
                wst.at[:, tile_cols(j, 1 - h)], wbuf.at[j, y, rows_of(z, c)],
                wx_send.at[j], wx_recv.at[0], d_n,
            ).wait_send()


def body(latents, timestep, gn_gain, gn_shift, temb_weight, w_query, w_keyval, w_out, stale_kv):
    vmem = pl.BlockSpec(memory_space=pltpu.VMEM)
    hbm = pl.BlockSpec(memory_space=pl.ANY)
    dma = pltpu.SemaphoreType.DMA
    phases = len(PHASES)
    scratch = [
        pltpu.VMEM((80, 4 * D), BF),
        pltpu.VMEM((5, NY, D, 128), BF),
        pltpu.VMEM((NZ, 2, 2, TOK, HALF), BF),
        pltpu.VMEM((2, TOK, D), BF),
        pltpu.VMEM((2 * TOK, D), F32),
        pltpu.VMEM((2 * TOK, D), BF),
        pltpu.VMEM((D, 128), BF),
        pltpu.VMEM((8, 128), F32),
        pltpu.VMEM((NZ - 1, 8, 128), F32),
        pltpu.VMEM((5, 256, 128), BF),
        pltpu.VMEM((5, 128, 128), BF),
        pltpu.VMEM((5, 128, 128), BF),
        pltpu.VMEM((5, 1, 256), F32),
        pltpu.VMEM((5, 1, 256), F32),
        pltpu.VMEM((5, 64, 256), F32),
        pltpu.VMEM((2 * TOK, D), BF),
        pltpu.VMEM((2, TOK, HALF), BF),
        pltpu.VMEM((TOK, HALF), BF),
        dma((3,)),
        dma((5,)), dma((phases,)),
        dma((phases, 7)), dma((phases, 7)),
        dma((phases, 8, 3)), dma((phases, 8, 3)),
        dma((phases, 8)), dma((phases, 8)),
        dma, dma,
        dma, dma,
        dma((7, 2)), dma((7, 2)),
        dma,
        dma((7,)), dma((7,)),
        dma((5,)), dma((5,)),
        dma, dma,
    ]
    return pl.pallas_call(
        kernel,
        out_shape=jax.ShapeDtypeStruct((TOK, D), BF),
        in_specs=[pl.BlockSpec(memory_space=pltpu.SMEM)] + [vmem] * 4 + [hbm] * 4,
        out_specs=vmem,
        scratch_shapes=scratch,
        compiler_params=pltpu.CompilerParams(
            collective_id=0, has_side_effects=True, vmem_limit_bytes=40 * 1024 * 1024
        ),
        name="midblock_attention",
    )(
        timestep, latents, gn_gain.reshape(1, D), gn_shift.reshape(1, D), temb_weight,
        w_query, w_keyval, w_out, stale_kv,
    )


def solution(mesh):
    in_specs = (
        P(("img", "patch"), None),
        P("img"),
        P(),
        P(),
        P(),
        P("patch", None),
        P("patch", None),
        P("patch", None),
        P(None, ("img", "patch"), None),
    )
    out_specs = P(("img", "patch"), None)
    return jax.shard_map(body, mesh=mesh, in_specs=in_specs, out_specs=out_specs, check_vma=False)
```

```python
import math

import jax
import jax.numpy as jnp
from jax import lax
from jax.experimental import pallas as pl
from jax.experimental.pallas import tpu as pltpu
from jax.sharding import PartitionSpec as P

MESH = pl.DeviceIdType.MESH
BF = jnp.bfloat16
F32 = jnp.float32
D = 1280
HALF = 640
TOK = 64
NZ = 8
NY = 4
GROUPS = 32
GROUP_WIDTH = D // GROUPS
TEMB = 320
EPS = 1e-06
PHASES = ((0, 2), (2, 5))
UNROLL = 5
DIRECT_Y = ()
EXP2_SCALE = 0.125 * math.log2(math.e)
NT = (((1,), (1,)), ((), ()))
TN = (((0,), (0,)), ((), ()))


def split3(x):
    high = x.astype(BF)
    rest = x - high.astype(F32)
    mid = rest.astype(BF)
    low = (rest - mid.astype(F32)).astype(BF)
    return [high, mid, low]


def stack_rows(rows, width):
    index = lax.broadcasted_iota(jnp.int32, (16, width), 0)
    out = jnp.zeros((16, width), F32)
    for k, row in enumerate(rows):
        out = jnp.where(index == k, jnp.broadcast_to(row.astype(F32), (16, width)), out)
    return out.astype(BF)


def kernel(
    ts_ref, lat_hbm, gain_hbm, shift_hbm, temb_hbm, wq_ref, wkv_ref, wo_ref, stale_ref,
    out_ref,
    lat_ref, gain_ref, shift_ref, temb_ref, wst, wxs, wbuf, kvbuf, latb, hid, normed, grp,
    stx, stb, q2, kfr, vfr, top_s, den_s, acc_s, att, mixs, mixr,
    ld_sem, wx_send, wx_recv, wz_send, wz_recv, wy_send, wy_recv, wc_send, wc_recv,
    lat_send, lat_recv, sx_send, sx_recv, sz_send, sz_recv, own_sem,
    stx_send, stx_recv, st_send, st_recv, at_send, at_recv, mx_send, mx_recv,
):
    img = lax.axis_index("img")
    patch = lax.axis_index("patch")
    xl, y, c = img // 8, (img // 2) % 4, img % 2
    z, h = patch // 2, patch % 2
    sgn = 1 - 2 * c

    def at_dev(xl_, y_, c_, z_, h_):
        return {"img": xl_ * 8 + y_ * 2 + c_, "patch": z_ * 2 + h_}

    def zmod(k):
        return (z + k + 2 * NZ) % NZ

    def ymod(k):
        return (y + k + 2 * NY) % NY

    d_zp, d_zm = at_dev(xl, y, c, zmod(sgn), h), at_dev(xl, y, c, zmod(-sgn), h)
    d_yp, d_ym = at_dev(xl, ymod(sgn), c, z, h), at_dev(xl, ymod(-sgn), c, z, h)
    d_c = at_dev(xl, y, 1 - c, z, h)
    d_x = at_dev(xl, y, c, z, 1 - h)
    d_n = at_dev(1 - xl, y, c, z, 1 - h)
    d_zpp, d_zmm = at_dev(xl, y, c, zmod(2 * sgn), h), at_dev(xl, y, c, zmod(-2 * sgn), h)
    d_nz = [at_dev(1 - xl, y, c, zmod(k * sgn), 1 - h) for k in (1, 2, -1, -2)]
    d_yy = at_dev(xl, ymod(2), c, z, h)

    sends = []

    def remote(src, dst, ssem, rsem, dev):
        return pltpu.make_async_remote_copy(
            src_ref=src, dst_ref=dst, send_sem=ssem, recv_sem=rsem, device_id=dev, device_id_type=MESH
        )

    def send(src, dst, ssem, rsem, dev):
        copy = remote(src, dst, ssem, rsem, dev)
        copy.start()
        sends.append(copy)

    def arrived(dst, ssem, rsem, dev):
        remote(dst, dst, ssem, rsem, dev).wait_recv()

    barrier = pltpu.get_barrier_semaphore()
    greeted = [d_zp, d_zm, d_zpp, d_zmm, d_yp, d_ym, d_yy, d_c, d_x, d_n] + d_nz
    for dev in greeted:
        pl.semaphore_signal(barrier, inc=1, device_id=dev, device_id_type=MESH)
    loads = [
        pltpu.make_async_copy(wq_ref, wst.at[:, 0:D], ld_sem.at[0]),
        pltpu.make_async_copy(wkv_ref, wst.at[:, D:3 * D], ld_sem.at[1]),
        pltpu.make_async_copy(wo_ref, wst.at[:, 3 * D:4 * D], ld_sem.at[2]),
        pltpu.make_async_copy(lat_hbm, lat_ref, ld_sem.at[3]),
        pltpu.make_async_copy(temb_hbm, temb_ref, ld_sem.at[4]),
        pltpu.make_async_copy(gain_hbm, gain_ref.at[0], ld_sem.at[5]),
        pltpu.make_async_copy(shift_hbm, shift_ref.at[0], ld_sem.at[6]),
    ]
    for copy in loads:
        copy.start()
    my_cols = pl.ds(pl.multiple_of(HALF * h, 128), HALF)
    other_cols = pl.ds(pl.multiple_of(HALF * (1 - h), 128), HALF)
    own_kv = pltpu.make_async_copy(stale_ref.at[:, :, my_cols], kvbuf.at[z, h], own_sem)
    own_kv.start()

    channel = lax.broadcasted_iota(jnp.int32, (D, 128), 0)
    first = lax.broadcasted_iota(jnp.int32, (D, 128), 1) * GROUP_WIDTH
    grp[...] = jnp.where((channel >= first) & (channel < first + GROUP_WIDTH), 1.0, 0.0).astype(BF)
    top_s[...] = jnp.full(top_s.shape, -jnp.inf, F32)
    den_s[...] = jnp.zeros(den_s.shape, F32)
    acc_s[...] = jnp.zeros(acc_s.shape, F32)
    for copy in loads:
        copy.wait()

    def rows_of(zz, cc):
        return pl.ds(pl.multiple_of(160 * zz + 80 * cc, 16), 80)

    def tile_cols(j, hh):
        t = 4 * j + y
        return pl.ds(pl.multiple_of(D * (t // 5) + HALF * hh + 128 * (t % 5), 128), 128)

    @pl.when(c == h)
    def _():
        for j in range(5):
            wbuf[j, y, rows_of(z, c)] = wst[:, tile_cols(j, h)]
            wxs[j] = wst[:, tile_cols(j, 1 - h)]

    latb[h] = lat_ref[...]

    lane = lax.broadcasted_iota(jnp.int32, (1, TEMB), 1)
    half = TEMB // 2
    k = jnp.where(lane < half, lane, lane - half).astype(F32)
    freqs = jnp.exp(-math.log(10000.0) * k / half)
    angles = ts_ref[0].astype(F32) * freqs
    embed = jnp.where(lane < half, jnp.cos(angles), jnp.sin(angles)).astype(BF)
    embed = stack_rows([embed], TEMB)
    pre = jnp.dot(embed, temb_ref[...], preferred_element_type=F32)[0:1]
    shift_vec = pre * (1.0 / (1.0 + jnp.exp(-pre)))

    pl.semaphore_wait(barrier, len(greeted))

    def unit(ph, yy, zz):
        j0, j1 = PHASES[ph]
        return wbuf.at[j0:j1, yy, rows_of(zz, c)]

    def zslot(m):
        return zmod(-sgn * m) if m <= 4 else zmod(sgn * (m - 4))

    def slots(tick):
        return [m for m in (tick, tick + 4 if 1 <= tick <= 3 else None) if m is not None]

    def z_forward(src, dst, ssem, rsem, m):
        if m <= 3:
            send(src, dst, ssem(m), rsem(m), d_zp)
        if m == 0 or 5 <= m <= 6:
            nxt = 4 if m == 0 else m
            send(src, dst, ssem(nxt), rsem(nxt), d_zm)

    def z_spread(src, dst, ssem, rsem, m):
        targets = {
            0: [(1, d_zp), (2, d_zpp), (5, d_zm), (6, d_zmm)],
            2: [(3, d_zp), (4, d_zpp)],
            6: [(7, d_zm)],
        }
        return [remote(src, dst(n), ssem(n), rsem(n), dev) for n, dev in targets.get(m, [])]

    def w_first_copies(ph):
        j0, j1 = PHASES[ph]
        ref, other = unit(ph, y, z), wxs.at[j0:j1]
        copies = [remote(other, ref, wx_send.at[ph, 0], wx_recv.at[ph], d_n)]
        for k, (n, dev) in enumerate(zip((1, 2, 5, 6), d_nz)):
            copies.append(remote(other, ref, wx_send.at[ph, 1 + k], wz_recv.at[ph, n - 1], dev))
        return copies + z_spread(
            ref, lambda n: ref, lambda n: wz_send.at[ph, n - 1], lambda n: wz_recv.at[ph, n - 1], 0
        )

    def w_first(ph):
        @pl.when(c == h)
        def _():
            for copy in w_first_copies(ph):
                copy.start()

    def w_own(ph):
        @pl.when(c != h)
        def _():
            arrived(unit(ph, y, z), wx_send.at[ph, 0], wx_recv.at[ph], d_n)

    def w_stage(ph, tick):
        for m in slots(tick):
            ref = unit(ph, y, zslot(m))
            arrived(ref, wz_send.at[ph, m - 1], wz_recv.at[ph, m - 1], d_zp)
            for copy in z_spread(
                ref, lambda n: ref, lambda n: wz_send.at[ph, n - 1], lambda n: wz_recv.at[ph, n - 1], m
            ):
                copy.start()
                sends.append(copy)

    def w_along_y(ph, tick):
        for m in slots(tick):
            ref = unit(ph, y, zslot(m))
            send(ref, ref, wy_send.at[ph, m, 0], wy_recv.at[ph, m, 0], d_yp)
            send(ref, ref, wy_send.at[ph, m, 1], wy_recv.at[ph, m, 1], d_ym)
            if ph in DIRECT_Y:
                send(ref, ref, wy_send.at[ph, m, 2], wy_recv.at[ph, m, 2], d_yy)

    def y_stage(ph, tick):
        for m in slots(tick):
            ref = unit(ph, ymod(-sgn), zslot(m))
            arrived(ref, wy_send.at[ph, m, 0], wy_recv.at[ph, m, 0], d_yp)
            if ph not in DIRECT_Y:
                send(ref, ref, wy_send.at[ph, m, 2], wy_recv.at[ph, m, 2], d_yp)

    def c_stage(ph, tick):
        j0, j1 = PHASES[ph]
        for m in slots(tick):
            zz = zslot(m)
            arrived(unit(ph, ymod(sgn), zz), wy_send.at[ph, m, 1], wy_recv.at[ph, m, 1], d_ym)
            arrived(unit(ph, ymod(2), zz), wy_send.at[ph, m, 2], wy_recv.at[ph, m, 2], d_yp)
            ref = wbuf.at[j0:j1, :, rows_of(zz, c)]
            send(ref, ref, wc_send.at[ph, m], wc_recv.at[ph, m], d_c)

    def w_ready(ph):
        j0, j1 = PHASES[ph]
        for m in range(8):
            zz = zmod(sgn * m) if m <= 4 else zmod(-sgn * (m - 4))
            arrived(wbuf.at[j0:j1, :, rows_of(zz, 1 - c)], wc_send.at[ph, m], wc_recv.at[ph, m], d_c)

    def s_stage(tick, part):
        for m in slots(tick):
            ref = kvbuf.at[zslot(m), h if part == 0 else 1 - h]
            src = ref
            if m == 0:
                if part == 0:
                    src = stale_ref.at[:, :, my_cols]
                else:
                    arrived(ref, sx_send, sx_recv, d_x)
            else:
                arrived(ref, sz_send.at[m - 1, part], sz_recv.at[m - 1, part], d_zp)
            z_forward(src, ref, lambda n: sz_send.at[n, part], lambda n: sz_recv.at[n, part], m)

    def send_latents():
        send(lat_ref, latb.at[h], lat_send, lat_recv, d_x)

    def send_stale():
        send(stale_ref.at[:, :, other_cols], kvbuf.at[z, h], sx_send, sx_recv, d_x)

    def group_sums(x):
        sums = jnp.dot(stack_rows(split3(x), D), grp[...], preferred_element_type=F32)
        return jnp.sum(sums, axis=0, keepdims=True)

    def to_channels(values):
        rows = []
        for v in values:
            rows += split3(v)
        spread = lax.dot_general(stack_rows(rows, 128), grp[...], NT, preferred_element_type=F32)
        return [jnp.sum(spread[3 * i:3 * i + 3], axis=0, keepdims=True) for i in range(len(values))]

    local_count = float(TOK * GROUP_WIDTH)
    total_count = 2 * NZ * local_count

    def own_stats():
        mine = pl.ds(pl.multiple_of(TOK * h, TOK), TOK)
        hidden = lat_ref[...].astype(F32) + shift_vec
        hid[mine] = hidden
        sums = group_sums(jnp.sum(hidden, axis=0, keepdims=True))
        (local_mean,) = to_channels([sums / local_count])
        centered = hidden - local_mean
        squares = group_sums(jnp.sum(centered * centered, axis=0, keepdims=True))
        stb[0, 0, 0:1] = sums
        stb[0, 0, 1:2] = squares
        send(stb.at[0, 0], stx, stx_send, stx_recv, d_x)

    def partner_hidden():
        arrived(latb.at[1 - h], lat_send, lat_recv, d_x)
        theirs = pl.ds(pl.multiple_of(TOK * (1 - h), TOK), TOK)
        hid[theirs] = latb[1 - h].astype(F32) + shift_vec

    def st_stage(tick):
        for m in slots(tick):
            if m == 0:
                arrived(stx, stx_send, stx_recv, d_x)
                stb[0, 1] = stx[...]
            else:
                arrived(stb.at[m], st_send.at[m - 1], st_recv.at[m - 1], d_zp)
            for copy in z_spread(
                stb.at[m], lambda n: stb.at[n], lambda n: st_send.at[n - 1], lambda n: st_recv.at[n - 1], m
            ):
                copy.start()
                sends.append(copy)

    def normalise():
        parts = [stb[m, n, 0:2] for m in range(NZ) for n in range(2)]
        mean = sum(part[0:1] for part in parts) / total_count
        total = jnp.zeros_like(mean)
        for part in parts:
            away = part[0:1] / local_count - mean
            total += part[1:2] + local_count * (away * away)
        rstd = lax.rsqrt(total / total_count + EPS)
        mean, rstd = to_channels([mean, rstd])
        gain, shift = gain_ref[...], shift_ref[...]
        for r in range(0, 2 * TOK, 16):
            scaled = (hid[r:r + 16] - mean) * rstd
            normed[r:r + 16] = (scaled * gain + shift).astype(BF)

    def weight_tile(t):
        return wbuf[t // 4, t % 4]

    q_lane = lax.broadcasted_iota(jnp.int32, (2 * TOK, 128), 1)

    def query_projection():
        for t in range(5):
            q = jnp.dot(normed[...], weight_tile(t), preferred_element_type=F32)
            q2[t, 0:128] = jnp.where(q_lane < 64, q, 0.0).astype(BF)
            q2[t, 128:256] = jnp.where(q_lane < 64, 0.0, q).astype(BF)

    def keyval_projection():
        for t in range(5):
            kfr[t] = jnp.dot(normed[...], weight_tile(5 + t), preferred_element_type=F32).astype(BF)
            vfr[t] = jnp.dot(normed[...], weight_tile(10 + t), preferred_element_type=F32).astype(BF)

    def blocks(q, key, value, mask=None):
        s = lax.dot_general(key, q, NT, preferred_element_type=F32)
        if mask is not None:
            s = jnp.where(mask, s, -jnp.inf)
        top = jnp.max(s, axis=0, keepdims=True)
        probs = jnp.exp2((s - top) * EXP2_SCALE).astype(BF)
        denom = jnp.sum(probs.astype(F32), axis=0, keepdims=True)
        both = lax.dot_general(value, probs, TN, preferred_element_type=F32)
        numer = jnp.concatenate([both[0:64, 0:128], both[64:128, 128:256]], axis=1)
        return top, numer, denom

    def merged(t, top, part_numer, part_denom):
        peak = top_s[t]
        new_peak = jnp.maximum(peak, top)
        keep = jnp.exp2((peak - new_peak) * EXP2_SCALE)
        weight = jnp.exp2((top - new_peak) * EXP2_SCALE)
        numer = acc_s[t] * keep + weight * part_numer
        denom = den_s[t] * keep + weight * part_denom
        return new_peak, numer, denom

    def merge(t, results):
        top_s[t], acc_s[t], den_s[t] = merged(t, *results)

    def stale_rows(zzs, which, cols):
        return jnp.concatenate([kvbuf[zz, xh, which, :, cols] for zz in zzs for xh in range(2)], axis=0)

    def stale_blocks(t, zzs):
        cols = pl.ds(pl.multiple_of(128 * t, 128), 128)
        return blocks(q2[t], stale_rows(zzs, 0, cols), stale_rows(zzs, 1, cols))

    def attend(zzs):
        def step(t, carry):
            merge(t, stale_blocks(t, zzs))
            return carry

        lax.fori_loop(0, 5, step, 0, unroll=UNROLL)

    def attend_own():
        own_kv.wait()
        row = lax.broadcasted_iota(jnp.int32, (256, 256), 0)
        block_of = (lax.broadcasted_iota(jnp.int32, (256, 256), 1) // TOK) % 2
        mask = (row < 128) == (((row // TOK) % 2) == block_of)

        def step(t, carry):
            cols = pl.ds(pl.multiple_of(128 * t, 128), 128)
            key = jnp.concatenate([kfr[t], stale_rows([z], 0, cols)], axis=0)
            value = jnp.concatenate([vfr[t], stale_rows([z], 1, cols)], axis=0)
            merge(t, blocks(q2[t], key, value, mask))
            return carry

        lax.fori_loop(0, 5, step, 0, unroll=UNROLL)

    def finish_attention(zz):
        for t in range(5):
            _, numer, denom = merged(t, *stale_blocks(t, [zz]))
            ratio = numer / denom
            turned = jnp.concatenate([ratio[:, 0:128], ratio[:, 128:256]], axis=0).T
            cols = pl.ds(pl.multiple_of(HALF * h + 128 * t, 128), 128)
            att[:, cols] = turned.astype(BF)
            send(att.at[:, cols], att.at[:, cols], at_send.at[t], at_recv.at[t], d_x)

    def output_projection():
        for t in range(5):
            cols = pl.ds(pl.multiple_of(HALF * (1 - h) + 128 * t, 128), 128)
            arrived(att.at[:, cols], at_send.at[t], at_recv.at[t], d_x)
        for who in (1 - h, h):
            rows = pl.ds(pl.multiple_of(TOK * who, TOK), TOK)
            attended = att[rows, :]
            for t in range(5):
                cols = pl.ds(pl.multiple_of(HALF * h + 128 * t, 128), 128)
                mixed = hid[rows, cols] + jnp.dot(attended, weight_tile(15 + t), preferred_element_type=F32)
                if who is h:
                    out_ref[:, cols] = mixed.astype(BF)
                else:
                    mixs[:, 128 * t:128 * t + 128] = mixed.astype(BF)
            if who is not h:
                send(mixs, mixr, mx_send, mx_recv, d_x)
        arrived(mixr, mx_send, mx_recv, d_x)
        out_ref[:, other_cols] = mixr[...]

    w_first(0)
    own_stats()
    w_first(1)
    w_own(0)
    w_own(1)
    w_along_y(0, 0)
    w_along_y(1, 0)
    w_stage(0, 2)
    st_stage(0)
    send_latents()
    w_stage(0, 1)
    w_along_y(0, 2)
    y_stage(0, 0)
    y_stage(1, 0)
    w_along_y(0, 1)
    w_stage(1, 2)
    send_stale()
    w_along_y(1, 2)
    w_stage(0, 3)
    st_stage(2)
    s_stage(0, 0)
    w_along_y(0, 3)
    c_stage(0, 0)
    y_stage(0, 2)
    w_stage(1, 4)
    w_stage(0, 4)
    s_stage(0, 1)
    w_along_y(0, 4)
    w_stage(1, 1)
    y_stage(0, 1)
    st_stage(3)
    w_stage(1, 3)
    s_stage(1, 0)
    y_stage(0, 3)
    c_stage(1, 0)
    w_along_y(1, 1)
    y_stage(0, 4)
    st_stage(1)
    partner_hidden()
    c_stage(0, 2)
    st_stage(4)
    w_along_y(1, 4)
    w_along_y(1, 3)
    c_stage(0, 3)
    y_stage(1, 2)
    s_stage(1, 1)
    s_stage(2, 0)
    y_stage(1, 4)
    c_stage(0, 1)
    c_stage(0, 4)
    y_stage(1, 3)
    y_stage(1, 1)
    w_ready(0)
    c_stage(1, 2)
    c_stage(1, 4)
    s_stage(2, 1)
    normalise()
    query_projection()
    c_stage(1, 3)
    c_stage(1, 1)
    s_stage(3, 0)
    attend([zslot(2), zslot(6)])
    attend([zslot(1), zslot(5)])
    w_ready(1)
    s_stage(3, 1)
    attend([zslot(3), zslot(7)])
    keyval_projection()
    attend_own()
    s_stage(4, 0)
    s_stage(4, 1)
    finish_attention(zslot(4))
    output_projection()

    for copy in sends:
        copy.wait_send()

    @pl.when(c == h)
    def _():
        for ph in range(len(PHASES)):
            for copy in w_first_copies(ph):
                copy.wait_send()


def body(latents, timestep, gn_gain, gn_shift, temb_weight, w_query, w_keyval, w_out, stale_kv):
    vmem = pl.BlockSpec(memory_space=pltpu.VMEM)
    hbm = pl.BlockSpec(memory_space=pl.ANY)
    dma = pltpu.SemaphoreType.DMA
    phases = len(PHASES)
    scratch = [
        pltpu.VMEM((TOK, D), BF),
        pltpu.VMEM((1, D), F32),
        pltpu.VMEM((1, D), F32),
        pltpu.VMEM((TEMB, D), BF),
        pltpu.VMEM((80, 4 * D), BF),
        pltpu.VMEM((5, 80, 128), BF),
        pltpu.VMEM((5, NY, D, 128), BF),
        pltpu.VMEM((NZ, 2, 2, TOK, HALF), BF),
        pltpu.VMEM((2, TOK, D), BF),
        pltpu.VMEM((2 * TOK, D), F32),
        pltpu.VMEM((2 * TOK, D), BF),
        pltpu.VMEM((D, 128), BF),
        pltpu.VMEM((8, 128), F32),
        pltpu.VMEM((NZ, 2, 8, 128), F32),
        pltpu.VMEM((5, 256, 128), BF),
        pltpu.VMEM((5, 128, 128), BF),
        pltpu.VMEM((5, 128, 128), BF),
        pltpu.VMEM((5, 1, 256), F32),
        pltpu.VMEM((5, 1, 256), F32),
        pltpu.VMEM((5, 64, 256), F32),
        pltpu.VMEM((2 * TOK, D), BF),
        pltpu.VMEM((TOK, HALF), BF),
        pltpu.VMEM((TOK, HALF), BF),
        dma((7,)),
        dma((phases, 5)), dma((phases,)),
        dma((phases, 7)), dma((phases, 7)),
        dma((phases, 8, 3)), dma((phases, 8, 3)),
        dma((phases, 8)), dma((phases, 8)),
        dma, dma,
        dma, dma,
        dma((7, 2)), dma((7, 2)),
        dma,
        dma, dma,
        dma((7,)), dma((7,)),
        dma((5,)), dma((5,)),
        dma, dma,
    ]
    return pl.pallas_call(
        kernel,
        out_shape=jax.ShapeDtypeStruct((TOK, D), BF),
        in_specs=[pl.BlockSpec(memory_space=pltpu.SMEM)] + [hbm] * 8,
        out_specs=vmem,
        scratch_shapes=scratch,
        compiler_params=pltpu.CompilerParams(
            collective_id=0, has_side_effects=True, vmem_limit_bytes=60 * 1024 * 1024
        ),
        name="midblock_attention",
    )(
        timestep, latents, gn_gain, gn_shift, temb_weight,
        w_query, w_keyval, w_out, stale_kv,
    )


def solution(mesh):
    in_specs = (
        P(("img", "patch"), None),
        P("img"),
        P(),
        P(),
        P(),
        P("patch", None),
        P("patch", None),
        P("patch", None),
        P(None, ("img", "patch"), None),
    )
    out_specs = P(("img", "patch"), None)
    return jax.shard_map(body, mesh=mesh, in_specs=in_specs, out_specs=out_specs, check_vma=False)
```

```python
import math

import jax
import jax.numpy as jnp
from jax import lax
from jax.experimental import pallas as pl
from jax.experimental.pallas import tpu as pltpu
from jax.sharding import PartitionSpec as P

MESH = pl.DeviceIdType.MESH
BF = jnp.bfloat16
F32 = jnp.float32
D = 1280
HALF = 640
TOK = 64
NZ = 8
NY = 4
GROUPS = 32
GROUP_WIDTH = D // GROUPS
TEMB = 320
EPS = 1e-06
PHASES = ((0, 5),)
UNROLL = 5
EXP2_SCALE = 0.125 * math.log2(math.e)
NT = (((1,), (1,)), ((), ()))
TN = (((0,), (0,)), ((), ()))


def split3(x):
    high = x.astype(BF)
    rest = x - high.astype(F32)
    mid = rest.astype(BF)
    low = (rest - mid.astype(F32)).astype(BF)
    return [high, mid, low]


def stack_rows(rows, width):
    index = lax.broadcasted_iota(jnp.int32, (16, width), 0)
    out = jnp.zeros((16, width), F32)
    for k, row in enumerate(rows):
        out = jnp.where(index == k, jnp.broadcast_to(row.astype(F32), (16, width)), out)
    return out.astype(BF)


def kernel(
    ts_ref, lat_hbm, gain_hbm, shift_hbm, temb_hbm, wq_ref, wkv_ref, wo_ref, stale_ref,
    out_ref,
    lat_ref, gain_ref, shift_ref, temb_ref, wst, wxs, wbuf, kvbuf, latb, hid, normed, grp,
    stx, stb, q2, kfr, vfr, top_s, den_s, acc_s, att, mixs, mixr,
    ld_sem, wx_send, wx_recv, wz_send, wz_recv, wy_send, wy_recv, wc_send, wc_recv,
    lat_send, lat_recv, sx_send, sx_recv, sz_send, sz_recv, own_sem,
    stx_send, stx_recv, st_send, st_recv, at_send, at_recv, mx_send, mx_recv,
):
    img = lax.axis_index("img")
    patch = lax.axis_index("patch")
    xl, y, c = img // 8, (img // 2) % 4, img % 2
    z, h = patch // 2, patch % 2
    sgn = 1 - 2 * c

    def at_dev(xl_, y_, c_, z_, h_):
        return {"img": xl_ * 8 + y_ * 2 + c_, "patch": z_ * 2 + h_}

    def zmod(k):
        return (z + k + 2 * NZ) % NZ

    def ymod(k):
        return (y + k + 2 * NY) % NY

    d_zp, d_zm = at_dev(xl, y, c, zmod(sgn), h), at_dev(xl, y, c, zmod(-sgn), h)
    d_yp, d_ym = at_dev(xl, ymod(sgn), c, z, h), at_dev(xl, ymod(-sgn), c, z, h)
    d_c = at_dev(xl, y, 1 - c, z, h)
    d_x = at_dev(xl, y, c, z, 1 - h)
    d_n = at_dev(1 - xl, y, c, z, 1 - h)
    d_nz = [at_dev(1 - xl, y, c, zmod(k * sgn), 1 - h) for k in (1, -1)]

    sends = []

    def remote(src, dst, ssem, rsem, dev):
        return pltpu.make_async_remote_copy(
            src_ref=src, dst_ref=dst, send_sem=ssem, recv_sem=rsem, device_id=dev, device_id_type=MESH
        )

    def send(src, dst, ssem, rsem, dev):
        copy = remote(src, dst, ssem, rsem, dev)
        copy.start()
        sends.append(copy)

    def arrived(dst, ssem, rsem, dev):
        remote(dst, dst, ssem, rsem, dev).wait_recv()

    barrier = pltpu.get_barrier_semaphore()
    greeted = [d_zp, d_zm, d_yp, d_ym, d_c, d_x, d_n] + d_nz
    for dev in greeted:
        pl.semaphore_signal(barrier, inc=1, device_id=dev, device_id_type=MESH)
    loads = [
        pltpu.make_async_copy(wq_ref, wst.at[:, 0:D], ld_sem.at[0]),
        pltpu.make_async_copy(wkv_ref, wst.at[:, D:3 * D], ld_sem.at[1]),
        pltpu.make_async_copy(wo_ref, wst.at[:, 3 * D:4 * D], ld_sem.at[2]),
        pltpu.make_async_copy(lat_hbm, lat_ref, ld_sem.at[3]),
        pltpu.make_async_copy(temb_hbm, temb_ref, ld_sem.at[4]),
        pltpu.make_async_copy(gain_hbm, gain_ref.at[0], ld_sem.at[5]),
        pltpu.make_async_copy(shift_hbm, shift_ref.at[0], ld_sem.at[6]),
    ]
    for copy in loads:
        copy.start()
    my_cols = pl.ds(pl.multiple_of(HALF * h, 128), HALF)
    other_cols = pl.ds(pl.multiple_of(HALF * (1 - h), 128), HALF)
    own_kv = pltpu.make_async_copy(stale_ref.at[:, :, my_cols], kvbuf.at[z, h], own_sem)
    own_kv.start()

    channel = lax.broadcasted_iota(jnp.int32, (D, 128), 0)
    first = lax.broadcasted_iota(jnp.int32, (D, 128), 1) * GROUP_WIDTH
    grp[...] = jnp.where((channel >= first) & (channel < first + GROUP_WIDTH), 1.0, 0.0).astype(BF)
    top_s[...] = jnp.full(top_s.shape, -jnp.inf, F32)
    den_s[...] = jnp.zeros(den_s.shape, F32)
    acc_s[...] = jnp.zeros(acc_s.shape, F32)
    for copy in loads:
        copy.wait()

    def rows_of(zz, cc):
        return pl.ds(pl.multiple_of(160 * zz + 80 * cc, 16), 80)

    def tile_cols(j, hh):
        t = 4 * j + y
        return pl.ds(pl.multiple_of(D * (t // 5) + HALF * hh + 128 * (t % 5), 128), 128)

    @pl.when(c == h)
    def _():
        for j in range(5):
            wbuf[j, y, rows_of(z, c)] = wst[:, tile_cols(j, h)]
            wxs[j] = wst[:, tile_cols(j, 1 - h)]

    latb[h] = lat_ref[...]

    lane = lax.broadcasted_iota(jnp.int32, (1, TEMB), 1)
    half = TEMB // 2
    k = jnp.where(lane < half, lane, lane - half).astype(F32)
    freqs = jnp.exp(-math.log(10000.0) * k / half)
    angles = ts_ref[0].astype(F32) * freqs
    embed = jnp.where(lane < half, jnp.cos(angles), jnp.sin(angles)).astype(BF)
    embed = stack_rows([embed], TEMB)
    pre = jnp.dot(embed, temb_ref[...], preferred_element_type=F32)[0:1]
    shift_vec = pre * (1.0 / (1.0 + jnp.exp(-pre)))

    pl.semaphore_wait(barrier, len(greeted))

    def unit(ph, yy, zz):
        j0, j1 = PHASES[ph]
        return wbuf.at[j0:j1, yy, rows_of(zz, c)]

    def zslot(m):
        return zmod(-sgn * m) if m <= 4 else zmod(sgn * (m - 4))

    def slots(tick):
        return [m for m in (tick, tick + 4 if 1 <= tick <= 3 else None) if m is not None]

    def z_forward(src, dst, ssem, rsem, m):
        if m <= 3:
            send(src, dst, ssem(m), rsem(m), d_zp)
        if m == 0 or 5 <= m <= 6:
            nxt = 4 if m == 0 else m
            send(src, dst, ssem(nxt), rsem(nxt), d_zm)

    def z_spread(src, dst, ssem, rsem, m):
        targets = {
            0: [(1, d_zp), (5, d_zm)], 1: [(2, d_zp)], 2: [(3, d_zp)], 3: [(4, d_zp)], 5: [(6, d_zm)], 6: [(7, d_zm)],
        }
        return [remote(src, dst(n), ssem(n), rsem(n), dev) for n, dev in targets.get(m, [])]

    def w_first_copies(ph):
        j0, j1 = PHASES[ph]
        ref, other = unit(ph, y, z), wxs.at[j0:j1]
        copies = [remote(other, ref, wx_send.at[ph, 0], wx_recv.at[ph], d_n)]
        for k, (n, dev) in enumerate(zip((1, 5), d_nz)):
            copies.append(remote(other, ref, wx_send.at[ph, 1 + k], wz_recv.at[ph, n - 1], dev))
        return copies + z_spread(
            ref, lambda n: ref, lambda n: wz_send.at[ph, n - 1], lambda n: wz_recv.at[ph, n - 1], 0
        )

    def w_first(ph):
        @pl.when(c == h)
        def _():
            for copy in w_first_copies(ph):
                copy.start()

    def w_own(ph):
        @pl.when(c != h)
        def _():
            arrived(unit(ph, y, z), wx_send.at[ph, 0], wx_recv.at[ph], d_n)

    def w_stage(ph, tick):
        for m in slots(tick):
            ref = unit(ph, y, zslot(m))
            arrived(ref, wz_send.at[ph, m - 1], wz_recv.at[ph, m - 1], d_zp)
            for copy in z_spread(
                ref, lambda n: ref, lambda n: wz_send.at[ph, n - 1], lambda n: wz_recv.at[ph, n - 1], m
            ):
                copy.start()
                sends.append(copy)

    def w_along_y(ph, tick):
        for m in slots(tick):
            ref = unit(ph, y, zslot(m))
            send(ref, ref, wy_send.at[ph, m, 0], wy_recv.at[ph, m, 0], d_yp)
            send(ref, ref, wy_send.at[ph, m, 1], wy_recv.at[ph, m, 1], d_ym)

    def y_stage(ph, tick):
        for m in slots(tick):
            ref = unit(ph, ymod(-sgn), zslot(m))
            arrived(ref, wy_send.at[ph, m, 0], wy_recv.at[ph, m, 0], d_yp)
            send(ref, ref, wy_send.at[ph, m, 2], wy_recv.at[ph, m, 2], d_yp)

    def c_stage(ph, tick):
        j0, j1 = PHASES[ph]
        for m in slots(tick):
            zz = zslot(m)
            arrived(unit(ph, ymod(sgn), zz), wy_send.at[ph, m, 1], wy_recv.at[ph, m, 1], d_ym)
            arrived(unit(ph, ymod(2), zz), wy_send.at[ph, m, 2], wy_recv.at[ph, m, 2], d_yp)
            ref = wbuf.at[j0:j1, :, rows_of(zz, c)]
            send(ref, ref, wc_send.at[ph, m], wc_recv.at[ph, m], d_c)

    def w_ready(ph):
        j0, j1 = PHASES[ph]
        for m in range(8):
            zz = zmod(sgn * m) if m <= 4 else zmod(-sgn * (m - 4))
            arrived(wbuf.at[j0:j1, :, rows_of(zz, 1 - c)], wc_send.at[ph, m], wc_recv.at[ph, m], d_c)

    def s_stage(tick, part):
        for m in slots(tick):
            ref = kvbuf.at[zslot(m), h if part == 0 else 1 - h]
            src = ref
            if m == 0:
                if part == 0:
                    src = stale_ref.at[:, :, my_cols]
                else:
                    arrived(ref, sx_send, sx_recv, d_x)
            else:
                arrived(ref, sz_send.at[m - 1, part], sz_recv.at[m - 1, part], d_zp)
            z_forward(src, ref, lambda n: sz_send.at[n, part], lambda n: sz_recv.at[n, part], m)

    def send_latents():
        send(lat_ref, latb.at[h], lat_send, lat_recv, d_x)

    def send_stale():
        send(stale_ref.at[:, :, other_cols], kvbuf.at[z, h], sx_send, sx_recv, d_x)

    def group_sums(x):
        sums = jnp.dot(stack_rows(split3(x), D), grp[...], preferred_element_type=F32)
        return jnp.sum(sums, axis=0, keepdims=True)

    def to_channels(values):
        rows = []
        for v in values:
            rows += split3(v)
        spread = lax.dot_general(stack_rows(rows, 128), grp[...], NT, preferred_element_type=F32)
        return [jnp.sum(spread[3 * i:3 * i + 3], axis=0, keepdims=True) for i in range(len(values))]

    local_count = float(TOK * GROUP_WIDTH)
    total_count = 2 * NZ * local_count

    def own_stats():
        mine = pl.ds(pl.multiple_of(TOK * h, TOK), TOK)
        hidden = lat_ref[...].astype(F32) + shift_vec
        hid[mine] = hidden
        sums = group_sums(jnp.sum(hidden, axis=0, keepdims=True))
        (local_mean,) = to_channels([sums / local_count])
        centered = hidden - local_mean
        squares = group_sums(jnp.sum(centered * centered, axis=0, keepdims=True))
        stb[0, 0, 0:1] = sums
        stb[0, 0, 1:2] = squares
        send(stb.at[0, 0], stx, stx_send, stx_recv, d_x)

    def partner_hidden():
        arrived(latb.at[1 - h], lat_send, lat_recv, d_x)
        theirs = pl.ds(pl.multiple_of(TOK * (1 - h), TOK), TOK)
        hid[theirs] = latb[1 - h].astype(F32) + shift_vec

    def st_stage(tick):
        for m in slots(tick):
            if m == 0:
                arrived(stx, stx_send, stx_recv, d_x)
                stb[0, 1] = stx[...]
            else:
                arrived(stb.at[m], st_send.at[m - 1], st_recv.at[m - 1], d_zp)
            for copy in z_spread(
                stb.at[m], lambda n: stb.at[n], lambda n: st_send.at[n - 1], lambda n: st_recv.at[n - 1], m
            ):
                copy.start()
                sends.append(copy)

    def normalise():
        parts = [stb[m, n, 0:2] for m in range(NZ) for n in range(2)]
        mean = sum(part[0:1] for part in parts) / total_count
        total = jnp.zeros_like(mean)
        for part in parts:
            away = part[0:1] / local_count - mean
            total += part[1:2] + local_count * (away * away)
        rstd = lax.rsqrt(total / total_count + EPS)
        mean, rstd = to_channels([mean, rstd])
        gain, shift = gain_ref[...], shift_ref[...]
        for r in range(0, 2 * TOK, 16):
            scaled = (hid[r:r + 16] - mean) * rstd
            normed[r:r + 16] = (scaled * gain + shift).astype(BF)

    def weight_tile(t):
        return wbuf[t // 4, t % 4]

    q_lane = lax.broadcasted_iota(jnp.int32, (2 * TOK, 128), 1)

    def query_projection():
        for t in range(5):
            q = jnp.dot(normed[...], weight_tile(t), preferred_element_type=F32)
            q2[t, 0:128] = jnp.where(q_lane < 64, q, 0.0).astype(BF)
            q2[t, 128:256] = jnp.where(q_lane < 64, 0.0, q).astype(BF)

    def keyval_projection():
        for t in range(5):
            kfr[t] = jnp.dot(normed[...], weight_tile(5 + t), preferred_element_type=F32).astype(BF)
            vfr[t] = jnp.dot(normed[...], weight_tile(10 + t), preferred_element_type=F32).astype(BF)

    def blocks(q, key, value, mask=None):
        s = lax.dot_general(key, q, NT, preferred_element_type=F32)
        if mask is not None:
            s = jnp.where(mask, s, -jnp.inf)
        top = jnp.max(s, axis=0, keepdims=True)
        probs = jnp.exp2((s - top) * EXP2_SCALE).astype(BF)
        denom = jnp.sum(probs.astype(F32), axis=0, keepdims=True)
        both = lax.dot_general(value, probs, TN, preferred_element_type=F32)
        numer = jnp.concatenate([both[0:64, 0:128], both[64:128, 128:256]], axis=1)
        return top, numer, denom

    def merged(t, top, part_numer, part_denom):
        peak = top_s[t]
        new_peak = jnp.maximum(peak, top)
        keep = jnp.exp2((peak - new_peak) * EXP2_SCALE)
        weight = jnp.exp2((top - new_peak) * EXP2_SCALE)
        numer = acc_s[t] * keep + weight * part_numer
        denom = den_s[t] * keep + weight * part_denom
        return new_peak, numer, denom

    def merge(t, results):
        top_s[t], acc_s[t], den_s[t] = merged(t, *results)

    def stale_rows(zzs, which, cols):
        return jnp.concatenate([kvbuf[zz, xh, which, :, cols] for zz in zzs for xh in range(2)], axis=0)

    def stale_blocks(t, zzs):
        cols = pl.ds(pl.multiple_of(128 * t, 128), 128)
        return blocks(q2[t], stale_rows(zzs, 0, cols), stale_rows(zzs, 1, cols))

    def attend(zzs):
        def step(t, carry):
            merge(t, stale_blocks(t, zzs))
            return carry

        lax.fori_loop(0, 5, step, 0, unroll=UNROLL)

    def attend_own():
        own_kv.wait()
        row = lax.broadcasted_iota(jnp.int32, (256, 256), 0)
        block_of = (lax.broadcasted_iota(jnp.int32, (256, 256), 1) // TOK) % 2
        mask = (row < 128) == (((row // TOK) % 2) == block_of)

        def step(t, carry):
            cols = pl.ds(pl.multiple_of(128 * t, 128), 128)
            key = jnp.concatenate([kfr[t], stale_rows([z], 0, cols)], axis=0)
            value = jnp.concatenate([vfr[t], stale_rows([z], 1, cols)], axis=0)
            merge(t, blocks(q2[t], key, value, mask))
            return carry

        lax.fori_loop(0, 5, step, 0, unroll=UNROLL)

    def finish_attention(zz):
        for t in range(5):
            _, numer, denom = merged(t, *stale_blocks(t, [zz]))
            ratio = numer / denom
            turned = jnp.concatenate([ratio[:, 0:128], ratio[:, 128:256]], axis=0).T
            cols = pl.ds(pl.multiple_of(HALF * h + 128 * t, 128), 128)
            att[:, cols] = turned.astype(BF)
            send(att.at[:, cols], att.at[:, cols], at_send.at[t], at_recv.at[t], d_x)

    def output_projection():
        own_rows = pl.ds(pl.multiple_of(HALF * h, 128), HALF)
        other_rows = pl.ds(pl.multiple_of(HALF * (1 - h), 128), HALF)

        def projected(attended, t, rows):
            return jnp.dot(attended, wbuf[(15 + t) // 4, (15 + t) % 4, rows], preferred_element_type=F32)

        attended = att[:, my_cols]
        for t in range(5):
            cols = pl.ds(pl.multiple_of(HALF * h + 128 * t, 128), 128)
            hid[:, cols] = hid[:, cols] + projected(attended, t, own_rows)
        for t in range(5):
            cols = pl.ds(pl.multiple_of(HALF * (1 - h) + 128 * t, 128), 128)
            arrived(att.at[:, cols], at_send.at[t], at_recv.at[t], d_x)
        for who in (1 - h, h):
            rows = pl.ds(pl.multiple_of(TOK * who, TOK), TOK)
            attended = att[rows, other_cols]
            for t in range(5):
                cols = pl.ds(pl.multiple_of(HALF * h + 128 * t, 128), 128)
                mixed = (hid[rows, cols] + projected(attended, t, other_rows)).astype(BF)
                if who is h:
                    out_ref[:, cols] = mixed
                else:
                    mixs[t] = mixed
                    send(mixs.at[t], mixr.at[t], mx_send.at[t], mx_recv.at[t], d_x)
        for t in range(5):
            cols = pl.ds(pl.multiple_of(HALF * (1 - h) + 128 * t, 128), 128)
            arrived(mixr.at[t], mx_send.at[t], mx_recv.at[t], d_x)
            out_ref[:, cols] = mixr[t]

    w_first(0)
    own_stats()
    w_own(0)
    w_along_y(0, 0)
    w_stage(0, 1)
    w_along_y(0, 1)
    st_stage(0)
    y_stage(0, 0)
    w_stage(0, 2)
    st_stage(1)
    send_latents()
    s_stage(0, 0)
    w_along_y(0, 2)
    w_stage(0, 3)
    w_along_y(0, 3)
    send_stale()
    st_stage(2)
    s_stage(1, 0)
    w_stage(0, 4)
    w_along_y(0, 4)
    y_stage(0, 2)
    y_stage(0, 1)
    s_stage(0, 1)
    st_stage(3)
    c_stage(0, 0)
    y_stage(0, 3)
    s_stage(2, 0)
    s_stage(1, 1)
    st_stage(4)
    partner_hidden()
    c_stage(0, 2)
    y_stage(0, 4)
    c_stage(0, 1)
    s_stage(3, 0)
    c_stage(0, 3)
    normalise()
    c_stage(0, 4)
    s_stage(2, 1)
    w_ready(0)
    query_projection()
    s_stage(4, 0)
    attend([zslot(1), zslot(5)])
    attend([zslot(2), zslot(6)])
    s_stage(3, 1)
    keyval_projection()
    attend_own()
    attend([zslot(3), zslot(7)])
    s_stage(4, 1)
    finish_attention(zslot(4))
    output_projection()

    for copy in sends:
        copy.wait_send()

    @pl.when(c == h)
    def _():
        for ph in range(len(PHASES)):
            for copy in w_first_copies(ph):
                copy.wait_send()


def body(latents, timestep, gn_gain, gn_shift, temb_weight, w_query, w_keyval, w_out, stale_kv):
    vmem = pl.BlockSpec(memory_space=pltpu.VMEM)
    hbm = pl.BlockSpec(memory_space=pl.ANY)
    dma = pltpu.SemaphoreType.DMA
    phases = len(PHASES)
    scratch = [
        pltpu.VMEM((TOK, D), BF),
        pltpu.VMEM((1, D), F32),
        pltpu.VMEM((1, D), F32),
        pltpu.VMEM((TEMB, D), BF),
        pltpu.VMEM((80, 4 * D), BF),
        pltpu.VMEM((5, 80, 128), BF),
        pltpu.VMEM((5, NY, D, 128), BF),
        pltpu.VMEM((NZ, 2, 2, TOK, HALF), BF),
        pltpu.VMEM((2, TOK, D), BF),
        pltpu.VMEM((2 * TOK, D), F32),
        pltpu.VMEM((2 * TOK, D), BF),
        pltpu.VMEM((D, 128), BF),
        pltpu.VMEM((8, 128), F32),
        pltpu.VMEM((NZ, 2, 8, 128), F32),
        pltpu.VMEM((5, 256, 128), BF),
        pltpu.VMEM((5, 128, 128), BF),
        pltpu.VMEM((5, 128, 128), BF),
        pltpu.VMEM((5, 1, 256), F32),
        pltpu.VMEM((5, 1, 256), F32),
        pltpu.VMEM((5, 64, 256), F32),
        pltpu.VMEM((2 * TOK, D), BF),
        pltpu.VMEM((5, TOK, 128), BF),
        pltpu.VMEM((5, TOK, 128), BF),
        dma((7,)),
        dma((phases, 3)), dma((phases,)),
        dma((phases, 7)), dma((phases, 7)),
        dma((phases, 8, 3)), dma((phases, 8, 3)),
        dma((phases, 8)), dma((phases, 8)),
        dma, dma,
        dma, dma,
        dma((7, 2)), dma((7, 2)),
        dma,
        dma, dma,
        dma((7,)), dma((7,)),
        dma((5,)), dma((5,)),
        dma((5,)), dma((5,)),
    ]
    return pl.pallas_call(
        kernel,
        out_shape=jax.ShapeDtypeStruct((TOK, D), BF),
        in_specs=[pl.BlockSpec(memory_space=pltpu.SMEM)] + [hbm] * 8,
        out_specs=vmem,
        scratch_shapes=scratch,
        compiler_params=pltpu.CompilerParams(
            collective_id=0, has_side_effects=True, vmem_limit_bytes=60 * 1024 * 1024
        ),
        name="midblock_attention",
    )(
        timestep, latents, gn_gain, gn_shift, temb_weight,
        w_query, w_keyval, w_out, stale_kv,
    )


def solution(mesh):
    in_specs = (
        P(("img", "patch"), None),
        P("img"),
        P(),
        P(),
        P(),
        P("patch", None),
        P("patch", None),
        P("patch", None),
        P(None, ("img", "patch"), None),
    )
    out_specs = P(("img", "patch"), None)
    return jax.shard_map(body, mesh=mesh, in_specs=in_specs, out_specs=out_specs, check_vma=False)
```

```python
import math

import jax
import jax.numpy as jnp
from jax import lax
from jax.experimental import pallas as pl
from jax.experimental.pallas import tpu as pltpu
from jax.sharding import PartitionSpec as P

MESH = pl.DeviceIdType.MESH
BF = jnp.bfloat16
F32 = jnp.float32
D = 1280
HALF = 640
TOK = 64
NZ = 8
NY = 4
GROUPS = 32
GROUP_WIDTH = D // GROUPS
TEMB = 320
EPS = 1e-06
PHASES = ((0, 5),)
UNROLL = 5
EXP2_SCALE = 0.125 * math.log2(math.e)
NT = (((1,), (1,)), ((), ()))
TN = (((0,), (0,)), ((), ()))


def split3(x):
    high = x.astype(BF)
    rest = x - high.astype(F32)
    mid = rest.astype(BF)
    low = (rest - mid.astype(F32)).astype(BF)
    return [high, mid, low]


def stack_rows(rows, width):
    index = lax.broadcasted_iota(jnp.int32, (16, width), 0)
    out = jnp.zeros((16, width), F32)
    for k, row in enumerate(rows):
        out = jnp.where(index == k, jnp.broadcast_to(row.astype(F32), (16, width)), out)
    return out.astype(BF)


def kernel(
    ts_ref, lat_hbm, gain_hbm, shift_hbm, temb_hbm, wq_ref, wkv_ref, wo_ref, stale_ref,
    out_ref,
    lat_ref, gain_ref, shift_ref, temb_ref, wst, wxs, wbuf, kvbuf, latb, hid, normed, grp,
    stx, stb, q2, kfr, vfr, top_s, den_s, acc_s, att, mixs, mixr,
    ld_sem, wx_send, wx_recv, wz_send, wz_recv, wy_send, wy_recv, wc_send, wc_recv,
    lat_send, lat_recv, sx_send, sx_recv, sz_send, sz_recv, own_sem,
    stx_send, stx_recv, st_send, st_recv, at_send, at_recv, mx_send, mx_recv,
):
    img = lax.axis_index("img")
    patch = lax.axis_index("patch")
    xl, y, c = img // 8, (img // 2) % 4, img % 2
    z, h = patch // 2, patch % 2
    sgn = 1 - 2 * c

    def at_dev(xl_, y_, c_, z_, h_):
        return {"img": xl_ * 8 + y_ * 2 + c_, "patch": z_ * 2 + h_}

    def zmod(k):
        return (z + k + 2 * NZ) % NZ

    def ymod(k):
        return (y + k + 2 * NY) % NY

    d_zp, d_zm = at_dev(xl, y, c, zmod(sgn), h), at_dev(xl, y, c, zmod(-sgn), h)
    d_yp, d_ym = at_dev(xl, ymod(sgn), c, z, h), at_dev(xl, ymod(-sgn), c, z, h)
    d_c = at_dev(xl, y, 1 - c, z, h)
    d_x = at_dev(xl, y, c, z, 1 - h)
    d_n = at_dev(1 - xl, y, c, z, 1 - h)
    d_nz = [at_dev(1 - xl, y, c, zmod(k * sgn), 1 - h) for k in (1, -1)]

    sends = []

    def remote(src, dst, ssem, rsem, dev):
        return pltpu.make_async_remote_copy(
            src_ref=src, dst_ref=dst, send_sem=ssem, recv_sem=rsem, device_id=dev, device_id_type=MESH
        )

    def send(src, dst, ssem, rsem, dev):
        copy = remote(src, dst, ssem, rsem, dev)
        copy.start()
        sends.append(copy)

    def arrived(dst, ssem, rsem, dev):
        remote(dst, dst, ssem, rsem, dev).wait_recv()

    barrier = pltpu.get_barrier_semaphore()
    greeted = [d_zp, d_zm, d_yp, d_ym, d_c, d_x, d_n] + d_nz
    for dev in greeted:
        pl.semaphore_signal(barrier, inc=1, device_id=dev, device_id_type=MESH)
    loads = [
        pltpu.make_async_copy(wq_ref, wst.at[:, 0:D], ld_sem.at[0]),
        pltpu.make_async_copy(wkv_ref, wst.at[:, D:3 * D], ld_sem.at[1]),
        pltpu.make_async_copy(wo_ref, wst.at[:, 3 * D:4 * D], ld_sem.at[2]),
        pltpu.make_async_copy(lat_hbm, lat_ref, ld_sem.at[3]),
        pltpu.make_async_copy(temb_hbm, temb_ref, ld_sem.at[4]),
        pltpu.make_async_copy(gain_hbm, gain_ref.at[0], ld_sem.at[5]),
        pltpu.make_async_copy(shift_hbm, shift_ref.at[0], ld_sem.at[6]),
    ]
    for copy in loads:
        copy.start()
    my_cols = pl.ds(pl.multiple_of(HALF * h, 128), HALF)
    other_cols = pl.ds(pl.multiple_of(HALF * (1 - h), 128), HALF)
    own_kv = pltpu.make_async_copy(stale_ref.at[:, :, my_cols], kvbuf.at[z, h], own_sem)
    own_kv.start()

    channel = lax.broadcasted_iota(jnp.int32, (D, 128), 0)
    first = lax.broadcasted_iota(jnp.int32, (D, 128), 1) * GROUP_WIDTH
    grp[...] = jnp.where((channel >= first) & (channel < first + GROUP_WIDTH), 1.0, 0.0).astype(BF)
    top_s[...] = jnp.full(top_s.shape, -jnp.inf, F32)
    den_s[...] = jnp.zeros(den_s.shape, F32)
    acc_s[...] = jnp.zeros(acc_s.shape, F32)
    for copy in loads:
        copy.wait()

    def rows_of(zz, cc):
        return pl.ds(pl.multiple_of(160 * zz + 80 * cc, 16), 80)

    def tile_cols(j, hh):
        t = 4 * j + y
        return pl.ds(pl.multiple_of(D * (t // 5) + HALF * hh + 128 * (t % 5), 128), 128)

    @pl.when(c == h)
    def _():
        for j in range(5):
            wbuf[j, y, rows_of(z, c)] = wst[:, tile_cols(j, h)]
            wxs[j] = wst[:, tile_cols(j, 1 - h)]

    latb[h] = lat_ref[...]

    lane = lax.broadcasted_iota(jnp.int32, (1, TEMB), 1)
    half = TEMB // 2
    k = jnp.where(lane < half, lane, lane - half).astype(F32)
    freqs = jnp.exp(-math.log(10000.0) * k / half)
    angles = ts_ref[0].astype(F32) * freqs
    embed = jnp.where(lane < half, jnp.cos(angles), jnp.sin(angles)).astype(BF)
    embed = stack_rows([embed], TEMB)
    pre = jnp.dot(embed, temb_ref[...], preferred_element_type=F32)[0:1]
    shift_vec = pre * (1.0 / (1.0 + jnp.exp(-pre)))

    pl.semaphore_wait(barrier, len(greeted))

    def unit(ph, yy, zz):
        j0, j1 = PHASES[ph]
        return wbuf.at[j0:j1, yy, rows_of(zz, c)]

    def zslot(m):
        return zmod(-sgn * m) if m <= 4 else zmod(sgn * (m - 4))

    def slots(tick):
        return [m for m in (tick, tick + 4 if 1 <= tick <= 3 else None) if m is not None]

    def z_forward(src, dst, ssem, rsem, m):
        if m <= 3:
            send(src, dst, ssem(m), rsem(m), d_zp)
        if m == 0 or 5 <= m <= 6:
            nxt = 4 if m == 0 else m
            send(src, dst, ssem(nxt), rsem(nxt), d_zm)

    def z_spread(src, dst, ssem, rsem, m):
        targets = {
            0: [(1, d_zp), (5, d_zm)], 1: [(2, d_zp)], 2: [(3, d_zp)], 3: [(4, d_zp)], 5: [(6, d_zm)], 6: [(7, d_zm)],
        }
        return [remote(src, dst(n), ssem(n), rsem(n), dev) for n, dev in targets.get(m, [])]

    def w_first_copies(ph):
        j0, j1 = PHASES[ph]
        ref, other = unit(ph, y, z), wxs.at[j0:j1]
        copies = [remote(other, ref, wx_send.at[ph, 0], wx_recv.at[ph], d_n)]
        for k, (n, dev) in enumerate(zip((1, 5), d_nz)):
            copies.append(remote(other, ref, wx_send.at[ph, 1 + k], wz_recv.at[ph, n - 1], dev))
        return copies + z_spread(
            ref, lambda n: ref, lambda n: wz_send.at[ph, n - 1], lambda n: wz_recv.at[ph, n - 1], 0
        )

    def w_first(ph):
        @pl.when(c == h)
        def _():
            for copy in w_first_copies(ph):
                copy.start()

    def w_own(ph):
        @pl.when(c != h)
        def _():
            arrived(unit(ph, y, z), wx_send.at[ph, 0], wx_recv.at[ph], d_n)

    def w_stage(ph, tick):
        for m in slots(tick):
            ref = unit(ph, y, zslot(m))
            arrived(ref, wz_send.at[ph, m - 1], wz_recv.at[ph, m - 1], d_zp)
            for copy in z_spread(
                ref, lambda n: ref, lambda n: wz_send.at[ph, n - 1], lambda n: wz_recv.at[ph, n - 1], m
            ):
                copy.start()
                sends.append(copy)

    def w_along_y(ph, tick):
        for m in slots(tick):
            ref = unit(ph, y, zslot(m))
            send(ref, ref, wy_send.at[ph, m, 0], wy_recv.at[ph, m, 0], d_yp)
            send(ref, ref, wy_send.at[ph, m, 1], wy_recv.at[ph, m, 1], d_ym)

    def y_stage(ph, tick):
        for m in slots(tick):
            ref = unit(ph, ymod(-sgn), zslot(m))
            arrived(ref, wy_send.at[ph, m, 0], wy_recv.at[ph, m, 0], d_yp)
            send(ref, ref, wy_send.at[ph, m, 2], wy_recv.at[ph, m, 2], d_yp)

    def c_stage(ph, tick):
        j0, j1 = PHASES[ph]
        for m in slots(tick):
            zz = zslot(m)
            arrived(unit(ph, ymod(sgn), zz), wy_send.at[ph, m, 1], wy_recv.at[ph, m, 1], d_ym)
            arrived(unit(ph, ymod(2), zz), wy_send.at[ph, m, 2], wy_recv.at[ph, m, 2], d_yp)
            ref = wbuf.at[j0:j1, :, rows_of(zz, c)]
            send(ref, ref, wc_send.at[ph, m], wc_recv.at[ph, m], d_c)

    def w_ready(ph):
        j0, j1 = PHASES[ph]
        for m in range(8):
            zz = zmod(sgn * m) if m <= 4 else zmod(-sgn * (m - 4))
            arrived(wbuf.at[j0:j1, :, rows_of(zz, 1 - c)], wc_send.at[ph, m], wc_recv.at[ph, m], d_c)

    def s_stage(tick, part):
        for m in slots(tick):
            ref = kvbuf.at[zslot(m), h if part == 0 else 1 - h]
            src = ref
            if m == 0:
                if part == 0:
                    src = stale_ref.at[:, :, my_cols]
                else:
                    arrived(ref, sx_send, sx_recv, d_x)
            else:
                arrived(ref, sz_send.at[m - 1, part], sz_recv.at[m - 1, part], d_zp)
            z_forward(src, ref, lambda n: sz_send.at[n, part], lambda n: sz_recv.at[n, part], m)

    def send_latents():
        send(lat_ref, latb.at[h], lat_send, lat_recv, d_x)

    def send_stale():
        send(stale_ref.at[:, :, other_cols], kvbuf.at[z, h], sx_send, sx_recv, d_x)

    def group_sums(x):
        sums = jnp.dot(stack_rows(split3(x), D), grp[...], preferred_element_type=F32)
        return jnp.sum(sums, axis=0, keepdims=True)

    def to_channels(values):
        rows = []
        for v in values:
            rows += split3(v)
        spread = lax.dot_general(stack_rows(rows, 128), grp[...], NT, preferred_element_type=F32)
        return [jnp.sum(spread[3 * i:3 * i + 3], axis=0, keepdims=True) for i in range(len(values))]

    local_count = float(TOK * GROUP_WIDTH)
    total_count = 2 * NZ * local_count

    def own_stats():
        mine = pl.ds(pl.multiple_of(TOK * h, TOK), TOK)
        hidden = lat_ref[...].astype(F32) + shift_vec
        hid[mine] = hidden
        sums = group_sums(jnp.sum(hidden, axis=0, keepdims=True))
        (local_mean,) = to_channels([sums / local_count])
        centered = hidden - local_mean
        squares = group_sums(jnp.sum(centered * centered, axis=0, keepdims=True))
        stb[0, 0, 0:1] = sums
        stb[0, 0, 1:2] = squares
        send(stb.at[0, 0], stx, stx_send, stx_recv, d_x)

    def partner_hidden():
        arrived(latb.at[1 - h], lat_send, lat_recv, d_x)
        theirs = pl.ds(pl.multiple_of(TOK * (1 - h), TOK), TOK)
        hid[theirs] = latb[1 - h].astype(F32) + shift_vec

    def st_stage(tick):
        for m in slots(tick):
            if m == 0:
                arrived(stx, stx_send, stx_recv, d_x)
                stb[0, 1] = stx[...]
            else:
                arrived(stb.at[m], st_send.at[m - 1], st_recv.at[m - 1], d_zp)
            for copy in z_spread(
                stb.at[m], lambda n: stb.at[n], lambda n: st_send.at[n - 1], lambda n: st_recv.at[n - 1], m
            ):
                copy.start()
                sends.append(copy)

    def normalise():
        parts = [stb[m, n, 0:2] for m in range(NZ) for n in range(2)]
        mean = sum(part[0:1] for part in parts) / total_count
        total = jnp.zeros_like(mean)
        for part in parts:
            away = part[0:1] / local_count - mean
            total += part[1:2] + local_count * (away * away)
        rstd = lax.rsqrt(total / total_count + EPS)
        mean, rstd = to_channels([mean, rstd])
        gain, shift = gain_ref[...], shift_ref[...]
        for r in range(0, 2 * TOK, 16):
            scaled = (hid[r:r + 16] - mean) * rstd
            normed[r:r + 16] = (scaled * gain + shift).astype(BF)

    def weight_tile(t):
        return wbuf[t // 4, t % 4]

    q_lane = lax.broadcasted_iota(jnp.int32, (2 * TOK, 128), 1)

    def query_projection():
        for t in range(5):
            q = jnp.dot(normed[...], weight_tile(t), preferred_element_type=F32)
            q2[t, 0:128] = jnp.where(q_lane < 64, q, 0.0).astype(BF)
            q2[t, 128:256] = jnp.where(q_lane < 64, 0.0, q).astype(BF)

    def keyval_projection():
        for t in range(5):
            kfr[t] = jnp.dot(normed[...], weight_tile(5 + t), preferred_element_type=F32).astype(BF)
            vfr[t] = jnp.dot(normed[...], weight_tile(10 + t), preferred_element_type=F32).astype(BF)

    def blocks(q, key, value, mask=None):
        s = lax.dot_general(key, q, NT, preferred_element_type=F32)
        if mask is not None:
            s = jnp.where(mask, s, -jnp.inf)
        top = jnp.max(s, axis=0, keepdims=True)
        probs = jnp.exp2((s - top) * EXP2_SCALE).astype(BF)
        denom = jnp.sum(probs.astype(F32), axis=0, keepdims=True)
        both = lax.dot_general(value, probs, TN, preferred_element_type=F32)
        numer = jnp.concatenate([both[0:64, 0:128], both[64:128, 128:256]], axis=1)
        return top, numer, denom

    def merged(t, top, part_numer, part_denom):
        peak = top_s[t]
        new_peak = jnp.maximum(peak, top)
        keep = jnp.exp2((peak - new_peak) * EXP2_SCALE)
        weight = jnp.exp2((top - new_peak) * EXP2_SCALE)
        numer = acc_s[t] * keep + weight * part_numer
        denom = den_s[t] * keep + weight * part_denom
        return new_peak, numer, denom

    def merge(t, results):
        top_s[t], acc_s[t], den_s[t] = merged(t, *results)

    def stale_rows(zzs, which, cols):
        return jnp.concatenate([kvbuf[zz, xh, which, :, cols] for zz in zzs for xh in range(2)], axis=0)

    def stale_blocks(t, zzs):
        cols = pl.ds(pl.multiple_of(128 * t, 128), 128)
        return blocks(q2[t], stale_rows(zzs, 0, cols), stale_rows(zzs, 1, cols))

    def attend(zzs):
        def step(t, carry):
            merge(t, stale_blocks(t, zzs))
            return carry

        lax.fori_loop(0, 5, step, 0, unroll=UNROLL)

    def attend_own():
        own_kv.wait()
        row = lax.broadcasted_iota(jnp.int32, (256, 256), 0)
        block_of = (lax.broadcasted_iota(jnp.int32, (256, 256), 1) // TOK) % 2
        mask = (row < 128) == (((row // TOK) % 2) == block_of)

        def step(t, carry):
            cols = pl.ds(pl.multiple_of(128 * t, 128), 128)
            key = jnp.concatenate([kfr[t], stale_rows([z], 0, cols)], axis=0)
            value = jnp.concatenate([vfr[t], stale_rows([z], 1, cols)], axis=0)
            merge(t, blocks(q2[t], key, value, mask))
            return carry

        lax.fori_loop(0, 5, step, 0, unroll=UNROLL)

    def finish_attention(zz):
        for t in range(5):
            _, numer, denom = merged(t, *stale_blocks(t, [zz]))
            ratio = numer / denom
            turned = jnp.concatenate([ratio[:, 0:128], ratio[:, 128:256]], axis=0).T
            cols = pl.ds(pl.multiple_of(HALF * h + 128 * t, 128), 128)
            att[:, cols] = turned.astype(BF)
            send(att.at[:, cols], att.at[:, cols], at_send.at[t], at_recv.at[t], d_x)

    def output_projection():
        own_rows = pl.ds(pl.multiple_of(HALF * h, 128), HALF)
        other_rows = pl.ds(pl.multiple_of(HALF * (1 - h), 128), HALF)

        def projected(attended, t, rows):
            return jnp.dot(attended, wbuf[(15 + t) // 4, (15 + t) % 4, rows], preferred_element_type=F32)

        attended = att[:, my_cols]
        for t in range(5):
            cols = pl.ds(pl.multiple_of(HALF * h + 128 * t, 128), 128)
            hid[:, cols] = hid[:, cols] + projected(attended, t, own_rows)
        for t in range(5):
            cols = pl.ds(pl.multiple_of(HALF * (1 - h) + 128 * t, 128), 128)
            arrived(att.at[:, cols], at_send.at[t], at_recv.at[t], d_x)
        for who in (1 - h, h):
            rows = pl.ds(pl.multiple_of(TOK * who, TOK), TOK)
            attended = att[rows, other_cols]
            for t in range(5):
                cols = pl.ds(pl.multiple_of(HALF * h + 128 * t, 128), 128)
                mixed = (hid[rows, cols] + projected(attended, t, other_rows)).astype(BF)
                if who is h:
                    out_ref[:, cols] = mixed
                else:
                    mixs[t] = mixed
                    send(mixs.at[t], mixr.at[t], mx_send.at[t], mx_recv.at[t], d_x)
        for t in range(5):
            cols = pl.ds(pl.multiple_of(HALF * (1 - h) + 128 * t, 128), 128)
            arrived(mixr.at[t], mx_send.at[t], mx_recv.at[t], d_x)
            out_ref[:, cols] = mixr[t]

    w_first(0)
    own_stats()
    w_own(0)
    w_along_y(0, 0)
    w_stage(0, 1)
    w_along_y(0, 1)
    st_stage(0)
    y_stage(0, 0)
    send_stale()
    w_stage(0, 2)
    st_stage(1)
    w_along_y(0, 2)
    s_stage(0, 0)
    send_latents()
    y_stage(0, 1)
    w_stage(0, 3)
    st_stage(2)
    w_along_y(0, 3)
    s_stage(0, 1)
    s_stage(1, 0)
    c_stage(0, 0)
    w_stage(0, 4)
    w_along_y(0, 4)
    y_stage(0, 2)
    s_stage(1, 1)
    c_stage(0, 1)
    st_stage(3)
    y_stage(0, 4)
    partner_hidden()
    s_stage(2, 0)
    y_stage(0, 3)
    c_stage(0, 2)
    s_stage(2, 1)
    c_stage(0, 4)
    st_stage(4)
    normalise()
    c_stage(0, 3)
    s_stage(3, 0)
    w_ready(0)
    query_projection()
    attend([zslot(2), zslot(6)])
    s_stage(3, 1)
    attend([zslot(1), zslot(5)])
    keyval_projection()
    attend([zslot(3), zslot(7)])
    attend_own()
    s_stage(4, 0)
    s_stage(4, 1)
    finish_attention(zslot(4))
    output_projection()

    for copy in sends:
        copy.wait_send()

    @pl.when(c == h)
    def _():
        for ph in range(len(PHASES)):
            for copy in w_first_copies(ph):
                copy.wait_send()


def body(latents, timestep, gn_gain, gn_shift, temb_weight, w_query, w_keyval, w_out, stale_kv):
    vmem = pl.BlockSpec(memory_space=pltpu.VMEM)
    hbm = pl.BlockSpec(memory_space=pl.ANY)
    dma = pltpu.SemaphoreType.DMA
    phases = len(PHASES)
    scratch = [
        pltpu.VMEM((TOK, D), BF),
        pltpu.VMEM((1, D), F32),
        pltpu.VMEM((1, D), F32),
        pltpu.VMEM((TEMB, D), BF),
        pltpu.VMEM((80, 4 * D), BF),
        pltpu.VMEM((5, 80, 128), BF),
        pltpu.VMEM((5, NY, D, 128), BF),
        pltpu.VMEM((NZ, 2, 2, TOK, HALF), BF),
        pltpu.VMEM((2, TOK, D), BF),
        pltpu.VMEM((2 * TOK, D), F32),
        pltpu.VMEM((2 * TOK, D), BF),
        pltpu.VMEM((D, 128), BF),
        pltpu.VMEM((8, 128), F32),
        pltpu.VMEM((NZ, 2, 8, 128), F32),
        pltpu.VMEM((5, 256, 128), BF),
        pltpu.VMEM((5, 128, 128), BF),
        pltpu.VMEM((5, 128, 128), BF),
        pltpu.VMEM((5, 1, 256), F32),
        pltpu.VMEM((5, 1, 256), F32),
        pltpu.VMEM((5, 64, 256), F32),
        pltpu.VMEM((2 * TOK, D), BF),
        pltpu.VMEM((5, TOK, 128), BF),
        pltpu.VMEM((5, TOK, 128), BF),
        dma((7,)),
        dma((phases, 3)), dma((phases,)),
        dma((phases, 7)), dma((phases, 7)),
        dma((phases, 8, 3)), dma((phases, 8, 3)),
        dma((phases, 8)), dma((phases, 8)),
        dma, dma,
        dma, dma,
        dma((7, 2)), dma((7, 2)),
        dma,
        dma, dma,
        dma((7,)), dma((7,)),
        dma((5,)), dma((5,)),
        dma((5,)), dma((5,)),
    ]
    return pl.pallas_call(
        kernel,
        out_shape=jax.ShapeDtypeStruct((TOK, D), BF),
        in_specs=[pl.BlockSpec(memory_space=pltpu.SMEM)] + [hbm] * 8,
        out_specs=vmem,
        scratch_shapes=scratch,
        compiler_params=pltpu.CompilerParams(
            collective_id=0, has_side_effects=True, vmem_limit_bytes=60 * 1024 * 1024
        ),
        name="midblock_attention",
    )(
        timestep, latents, gn_gain, gn_shift, temb_weight,
        w_query, w_keyval, w_out, stale_kv,
    )


def solution(mesh):
    in_specs = (
        P(("img", "patch"), None),
        P("img"),
        P(),
        P(),
        P(),
        P("patch", None),
        P("patch", None),
        P("patch", None),
        P(None, ("img", "patch"), None),
    )
    out_specs = P(("img", "patch"), None)
    return jax.shard_map(body, mesh=mesh, in_specs=in_specs, out_specs=out_specs, check_vma=False)
```

```python
import math

import jax
import jax.numpy as jnp
from jax import lax
from jax.experimental import pallas as pl
from jax.experimental.pallas import tpu as pltpu
from jax.sharding import PartitionSpec as P

MESH = pl.DeviceIdType.MESH
BF = jnp.bfloat16
F32 = jnp.float32
D = 1280
HALF = 640
TOK = 64
NZ = 8
NY = 4
GROUPS = 32
GROUP_WIDTH = D // GROUPS
TEMB = 320
EPS = 1e-06
PHASES = ((0, 5),)
UNROLL = 5
EXP2_SCALE = 0.125 * math.log2(math.e)
NT = (((1,), (1,)), ((), ()))
TN = (((0,), (0,)), ((), ()))


def split3(x):
    high = x.astype(BF)
    rest = x - high.astype(F32)
    mid = rest.astype(BF)
    low = (rest - mid.astype(F32)).astype(BF)
    return [high, mid, low]


def stack_rows(rows, width):
    index = lax.broadcasted_iota(jnp.int32, (16, width), 0)
    out = jnp.zeros((16, width), F32)
    for k, row in enumerate(rows):
        out = jnp.where(index == k, jnp.broadcast_to(row.astype(F32), (16, width)), out)
    return out.astype(BF)


def kernel(
    ts_ref, lat_hbm, gain_hbm, shift_hbm, temb_hbm, wq_ref, wkv_ref, wo_ref, stale_ref,
    out_ref,
    lat_ref, gain_ref, shift_ref, temb_ref, wst, wxs, wbuf, kvbuf, latb, hid, normed, grp,
    stx, stb, q2, kfr, vfr, top_s, den_s, acc_s, att, mixs, mixr,
    ld_sem, wx_send, wx_recv, wz_send, wz_recv, wy_send, wy_recv, wc_send, wc_recv,
    lat_send, lat_recv, sx_send, sx_recv, sz_send, sz_recv, own_sem,
    stx_send, stx_recv, st_send, st_recv, at_send, at_recv, mx_send, mx_recv,
):
    img = lax.axis_index("img")
    patch = lax.axis_index("patch")
    xl, y, c = img // 8, (img // 2) % 4, img % 2
    z, h = patch // 2, patch % 2
    sgn = 1 - 2 * c

    def at_dev(xl_, y_, c_, z_, h_):
        return {"img": xl_ * 8 + y_ * 2 + c_, "patch": z_ * 2 + h_}

    def zmod(k):
        return (z + k + 2 * NZ) % NZ

    def ymod(k):
        return (y + k + 2 * NY) % NY

    d_zp, d_zm = at_dev(xl, y, c, zmod(sgn), h), at_dev(xl, y, c, zmod(-sgn), h)
    d_yp, d_ym = at_dev(xl, ymod(sgn), c, z, h), at_dev(xl, ymod(-sgn), c, z, h)
    d_c = at_dev(xl, y, 1 - c, z, h)
    d_x = at_dev(xl, y, c, z, 1 - h)
    d_n = at_dev(1 - xl, y, c, z, 1 - h)
    d_nz = [at_dev(1 - xl, y, c, zmod(k * sgn), 1 - h) for k in (1, -1)]

    sends = []

    def remote(src, dst, ssem, rsem, dev):
        return pltpu.make_async_remote_copy(
            src_ref=src, dst_ref=dst, send_sem=ssem, recv_sem=rsem, device_id=dev, device_id_type=MESH
        )

    def send(src, dst, ssem, rsem, dev):
        copy = remote(src, dst, ssem, rsem, dev)
        copy.start()
        sends.append(copy)

    def arrived(dst, ssem, rsem, dev):
        remote(dst, dst, ssem, rsem, dev).wait_recv()

    barrier = pltpu.get_barrier_semaphore()
    greeted = [d_zp, d_zm, d_yp, d_ym, d_c, d_x, d_n] + d_nz
    for dev in greeted:
        pl.semaphore_signal(barrier, inc=1, device_id=dev, device_id_type=MESH)
    loads = [
        pltpu.make_async_copy(wq_ref, wst.at[:, 0:D], ld_sem.at[0]),
        pltpu.make_async_copy(wkv_ref, wst.at[:, D:3 * D], ld_sem.at[1]),
        pltpu.make_async_copy(wo_ref, wst.at[:, 3 * D:4 * D], ld_sem.at[2]),
        pltpu.make_async_copy(lat_hbm, lat_ref, ld_sem.at[3]),
        pltpu.make_async_copy(temb_hbm, temb_ref, ld_sem.at[4]),
        pltpu.make_async_copy(gain_hbm, gain_ref.at[0], ld_sem.at[5]),
        pltpu.make_async_copy(shift_hbm, shift_ref.at[0], ld_sem.at[6]),
    ]
    for copy in loads:
        copy.start()
    my_cols = pl.ds(pl.multiple_of(HALF * h, 128), HALF)
    other_cols = pl.ds(pl.multiple_of(HALF * (1 - h), 128), HALF)
    own_kv = pltpu.make_async_copy(stale_ref.at[:, :, my_cols], kvbuf.at[z, h], own_sem)
    own_kv.start()

    channel = lax.broadcasted_iota(jnp.int32, (D, 128), 0)
    first = lax.broadcasted_iota(jnp.int32, (D, 128), 1) * GROUP_WIDTH
    grp[...] = jnp.where((channel >= first) & (channel < first + GROUP_WIDTH), 1.0, 0.0).astype(BF)
    top_s[...] = jnp.full(top_s.shape, -jnp.inf, F32)
    den_s[...] = jnp.zeros(den_s.shape, F32)
    acc_s[...] = jnp.zeros(acc_s.shape, F32)
    for copy in loads:
        copy.wait()

    def rows_of(zz, cc):
        return pl.ds(pl.multiple_of(160 * zz + 80 * cc, 16), 80)

    def tile_cols(j, hh):
        t = 4 * j + y
        return pl.ds(pl.multiple_of(D * (t // 5) + HALF * hh + 128 * (t % 5), 128), 128)

    @pl.when(c == h)
    def _():
        for j in range(5):
            wbuf[j, y, rows_of(z, c)] = wst[:, tile_cols(j, h)]
            wxs[j] = wst[:, tile_cols(j, 1 - h)]

    latb[h] = lat_ref[...]

    lane = lax.broadcasted_iota(jnp.int32, (1, TEMB), 1)
    half = TEMB // 2
    k = jnp.where(lane < half, lane, lane - half).astype(F32)
    freqs = jnp.exp(-math.log(10000.0) * k / half)
    angles = ts_ref[0].astype(F32) * freqs
    embed = jnp.where(lane < half, jnp.cos(angles), jnp.sin(angles)).astype(BF)
    embed = stack_rows([embed], TEMB)
    pre = jnp.dot(embed, temb_ref[...], preferred_element_type=F32)[0:1]
    shift_vec = pre * (1.0 / (1.0 + jnp.exp(-pre)))

    pl.semaphore_wait(barrier, len(greeted))

    def unit(ph, yy, zz):
        j0, j1 = PHASES[ph]
        return wbuf.at[j0:j1, yy, rows_of(zz, c)]

    def zslot(m):
        return zmod(-sgn * m) if m <= 4 else zmod(sgn * (m - 4))

    def slots(tick):
        return [m for m in (tick, tick + 4 if 1 <= tick <= 3 else None) if m is not None]

    def z_forward(src, dst, ssem, rsem, m):
        if m <= 3:
            send(src, dst, ssem(m), rsem(m), d_zp)
        if m == 0 or 5 <= m <= 6:
            nxt = 4 if m == 0 else m
            send(src, dst, ssem(nxt), rsem(nxt), d_zm)

    def z_spread(src, dst, ssem, rsem, m):
        targets = {
            0: [(1, d_zp), (5, d_zm)], 1: [(2, d_zp)], 2: [(3, d_zp)], 3: [(4, d_zp)], 5: [(6, d_zm)], 6: [(7, d_zm)],
        }
        return [remote(src, dst(n), ssem(n), rsem(n), dev) for n, dev in targets.get(m, [])]

    def w_first_copies(ph):
        j0, j1 = PHASES[ph]
        ref, other = unit(ph, y, z), wxs.at[j0:j1]
        copies = [remote(other, ref, wx_send.at[ph, 0], wx_recv.at[ph], d_n)]
        for k, (n, dev) in enumerate(zip((1, 5), d_nz)):
            copies.append(remote(other, ref, wx_send.at[ph, 1 + k], wz_recv.at[ph, n - 1], dev))
        return copies + z_spread(
            ref, lambda n: ref, lambda n: wz_send.at[ph, n - 1], lambda n: wz_recv.at[ph, n - 1], 0
        )

    def w_first(ph):
        @pl.when(c == h)
        def _():
            for copy in w_first_copies(ph):
                copy.start()

    def w_own(ph):
        @pl.when(c != h)
        def _():
            arrived(unit(ph, y, z), wx_send.at[ph, 0], wx_recv.at[ph], d_n)

    def w_stage(ph, tick):
        for m in slots(tick):
            ref = unit(ph, y, zslot(m))
            arrived(ref, wz_send.at[ph, m - 1], wz_recv.at[ph, m - 1], d_zp)
            for copy in z_spread(
                ref, lambda n: ref, lambda n: wz_send.at[ph, n - 1], lambda n: wz_recv.at[ph, n - 1], m
            ):
                copy.start()
                sends.append(copy)

    def w_along_y(ph, tick):
        for m in slots(tick):
            ref = unit(ph, y, zslot(m))
            send(ref, ref, wy_send.at[ph, m, 0], wy_recv.at[ph, m, 0], d_yp)
            send(ref, ref, wy_send.at[ph, m, 1], wy_recv.at[ph, m, 1], d_ym)

    def y_stage(ph, tick):
        for m in slots(tick):
            ref = unit(ph, ymod(-sgn), zslot(m))
            arrived(ref, wy_send.at[ph, m, 0], wy_recv.at[ph, m, 0], d_yp)
            send(ref, ref, wy_send.at[ph, m, 2], wy_recv.at[ph, m, 2], d_yp)

    def c_stage(ph, tick):
        j0, j1 = PHASES[ph]
        for m in slots(tick):
            zz = zslot(m)
            arrived(unit(ph, ymod(sgn), zz), wy_send.at[ph, m, 1], wy_recv.at[ph, m, 1], d_ym)
            arrived(unit(ph, ymod(2), zz), wy_send.at[ph, m, 2], wy_recv.at[ph, m, 2], d_yp)
            ref = wbuf.at[j0:j1, :, rows_of(zz, c)]
            send(ref, ref, wc_send.at[ph, m], wc_recv.at[ph, m], d_c)

    def w_ready(ph):
        j0, j1 = PHASES[ph]
        for m in range(8):
            zz = zmod(sgn * m) if m <= 4 else zmod(-sgn * (m - 4))
            arrived(wbuf.at[j0:j1, :, rows_of(zz, 1 - c)], wc_send.at[ph, m], wc_recv.at[ph, m], d_c)

    def s_stage(tick, part):
        for m in slots(tick):
            ref = kvbuf.at[zslot(m), h if part == 0 else 1 - h]
            src = ref
            if m == 0:
                if part == 0:
                    src = stale_ref.at[:, :, my_cols]
                else:
                    arrived(ref, sx_send, sx_recv, d_x)
            else:
                arrived(ref, sz_send.at[m - 1, part], sz_recv.at[m - 1, part], d_zp)
            z_forward(src, ref, lambda n: sz_send.at[n, part], lambda n: sz_recv.at[n, part], m)

    def send_latents():
        send(lat_ref, latb.at[h], lat_send, lat_recv, d_x)

    def send_stale():
        send(stale_ref.at[:, :, other_cols], kvbuf.at[z, h], sx_send, sx_recv, d_x)

    def group_sums(x):
        sums = jnp.dot(stack_rows(split3(x), D), grp[...], preferred_element_type=F32)
        return jnp.sum(sums, axis=0, keepdims=True)

    def to_channels(values):
        rows = []
        for v in values:
            rows += split3(v)
        spread = lax.dot_general(stack_rows(rows, 128), grp[...], NT, preferred_element_type=F32)
        return [jnp.sum(spread[3 * i:3 * i + 3], axis=0, keepdims=True) for i in range(len(values))]

    local_count = float(TOK * GROUP_WIDTH)
    total_count = 2 * NZ * local_count

    def own_stats():
        mine = pl.ds(pl.multiple_of(TOK * h, TOK), TOK)
        hidden = lat_ref[...].astype(F32) + shift_vec
        hid[mine] = hidden
        sums = group_sums(jnp.sum(hidden, axis=0, keepdims=True))
        (local_mean,) = to_channels([sums / local_count])
        centered = hidden - local_mean
        squares = group_sums(jnp.sum(centered * centered, axis=0, keepdims=True))
        stb[0, 0, 0:1] = sums
        stb[0, 0, 1:2] = squares
        send(stb.at[0, 0], stx, stx_send, stx_recv, d_x)

    def partner_hidden():
        arrived(latb.at[1 - h], lat_send, lat_recv, d_x)
        theirs = pl.ds(pl.multiple_of(TOK * (1 - h), TOK), TOK)
        hid[theirs] = latb[1 - h].astype(F32) + shift_vec

    def st_stage(tick):
        for m in slots(tick):
            if m == 0:
                arrived(stx, stx_send, stx_recv, d_x)
                stb[0, 1] = stx[...]
            else:
                arrived(stb.at[m], st_send.at[m - 1], st_recv.at[m - 1], d_zp)
            for copy in z_spread(
                stb.at[m], lambda n: stb.at[n], lambda n: st_send.at[n - 1], lambda n: st_recv.at[n - 1], m
            ):
                copy.start()
                sends.append(copy)

    def normalise():
        parts = [stb[m, n, 0:2] for m in range(NZ) for n in range(2)]
        mean = sum(part[0:1] for part in parts) / total_count
        total = jnp.zeros_like(mean)
        for part in parts:
            away = part[0:1] / local_count - mean
            total += part[1:2] + local_count * (away * away)
        rstd = lax.rsqrt(total / total_count + EPS)
        mean, rstd = to_channels([mean, rstd])
        gain, shift = gain_ref[...], shift_ref[...]
        for r in range(0, 2 * TOK, 16):
            scaled = (hid[r:r + 16] - mean) * rstd
            normed[r:r + 16] = (scaled * gain + shift).astype(BF)

    def weight_tile(t):
        return wbuf[t // 4, t % 4]

    q_lane = lax.broadcasted_iota(jnp.int32, (2 * TOK, 128), 1)

    def query_projection():
        for t in range(5):
            q = jnp.dot(normed[...], weight_tile(t), preferred_element_type=F32)
            q2[t, 0:128] = jnp.where(q_lane < 64, q, 0.0).astype(BF)
            q2[t, 128:256] = jnp.where(q_lane < 64, 0.0, q).astype(BF)

    def keyval_projection():
        for t in range(5):
            kfr[t] = jnp.dot(normed[...], weight_tile(5 + t), preferred_element_type=F32).astype(BF)
            vfr[t] = jnp.dot(normed[...], weight_tile(10 + t), preferred_element_type=F32).astype(BF)

    def blocks(q, key, value, mask=None):
        s = lax.dot_general(key, q, NT, preferred_element_type=F32)
        if mask is not None:
            s = jnp.where(mask, s, -jnp.inf)
        top = jnp.max(s, axis=0, keepdims=True)
        probs = jnp.exp2((s - top) * EXP2_SCALE).astype(BF)
        denom = jnp.sum(probs.astype(F32), axis=0, keepdims=True)
        both = lax.dot_general(value, probs, TN, preferred_element_type=F32)
        numer = jnp.concatenate([both[0:64, 0:128], both[64:128, 128:256]], axis=1)
        return top, numer, denom

    def merged(t, top, part_numer, part_denom):
        peak = top_s[t]
        new_peak = jnp.maximum(peak, top)
        keep = jnp.exp2((peak - new_peak) * EXP2_SCALE)
        weight = jnp.exp2((top - new_peak) * EXP2_SCALE)
        numer = acc_s[t] * keep + weight * part_numer
        denom = den_s[t] * keep + weight * part_denom
        return new_peak, numer, denom

    def merge(t, results):
        top_s[t], acc_s[t], den_s[t] = merged(t, *results)

    def stale_rows(zzs, which, cols):
        return jnp.concatenate([kvbuf[zz, xh, which, :, cols] for zz in zzs for xh in range(2)], axis=0)

    def stale_blocks(t, zzs):
        cols = pl.ds(pl.multiple_of(128 * t, 128), 128)
        return blocks(q2[t], stale_rows(zzs, 0, cols), stale_rows(zzs, 1, cols))

    def attend(zzs):
        def step(t, carry):
            merge(t, stale_blocks(t, zzs))
            return carry

        lax.fori_loop(0, 5, step, 0, unroll=UNROLL)

    def attend_own():
        own_kv.wait()
        row = lax.broadcasted_iota(jnp.int32, (256, 256), 0)
        block_of = (lax.broadcasted_iota(jnp.int32, (256, 256), 1) // TOK) % 2
        mask = (row < 128) == (((row // TOK) % 2) == block_of)

        def step(t, carry):
            cols = pl.ds(pl.multiple_of(128 * t, 128), 128)
            key = jnp.concatenate([kfr[t], stale_rows([z], 0, cols)], axis=0)
            value = jnp.concatenate([vfr[t], stale_rows([z], 1, cols)], axis=0)
            merge(t, blocks(q2[t], key, value, mask))
            return carry

        lax.fori_loop(0, 5, step, 0, unroll=UNROLL)

    def finish_attention(zz):
        for t in range(5):
            _, numer, denom = merged(t, *stale_blocks(t, [zz]))
            ratio = numer / denom
            turned = jnp.concatenate([ratio[:, 0:128], ratio[:, 128:256]], axis=0).T
            cols = pl.ds(pl.multiple_of(HALF * h + 128 * t, 128), 128)
            att[:, cols] = turned.astype(BF)
            send(att.at[:, cols], att.at[:, cols], at_send.at[t], at_recv.at[t], d_x)

    def output_projection():
        own_rows = pl.ds(pl.multiple_of(HALF * h, 128), HALF)
        other_rows = pl.ds(pl.multiple_of(HALF * (1 - h), 128), HALF)

        def projected(attended, t, rows):
            return jnp.dot(attended, wbuf[(15 + t) // 4, (15 + t) % 4, rows], preferred_element_type=F32)

        attended = att[:, my_cols]
        for t in range(5):
            cols = pl.ds(pl.multiple_of(HALF * h + 128 * t, 128), 128)
            hid[:, cols] = hid[:, cols] + projected(attended, t, own_rows)
        for t in range(5):
            cols = pl.ds(pl.multiple_of(HALF * (1 - h) + 128 * t, 128), 128)
            arrived(att.at[:, cols], at_send.at[t], at_recv.at[t], d_x)
        for who in (1 - h, h):
            rows = pl.ds(pl.multiple_of(TOK * who, TOK), TOK)
            attended = att[rows, other_cols]
            for t in range(5):
                cols = pl.ds(pl.multiple_of(HALF * h + 128 * t, 128), 128)
                mixed = (hid[rows, cols] + projected(attended, t, other_rows)).astype(BF)
                if who is h:
                    out_ref[:, cols] = mixed
                else:
                    mixs[t] = mixed
                    send(mixs.at[t], mixr.at[t], mx_send.at[t], mx_recv.at[t], d_x)
        for t in range(5):
            cols = pl.ds(pl.multiple_of(HALF * (1 - h) + 128 * t, 128), 128)
            arrived(mixr.at[t], mx_send.at[t], mx_recv.at[t], d_x)
            out_ref[:, cols] = mixr[t]

    w_first(0)
    own_stats()
    w_own(0)
    w_along_y(0, 0)
    w_stage(0, 1)
    w_along_y(0, 1)
    send_stale()
    s_stage(0, 0)
    st_stage(0)
    y_stage(0, 0)
    w_stage(0, 2)
    w_along_y(0, 2)
    s_stage(1, 0)
    y_stage(0, 1)
    st_stage(1)
    w_stage(0, 3)
    w_along_y(0, 3)
    c_stage(0, 0)
    send_latents()
    s_stage(0, 1)
    st_stage(2)
    w_stage(0, 4)
    w_along_y(0, 4)
    y_stage(0, 2)
    s_stage(1, 1)
    st_stage(3)
    s_stage(2, 0)
    partner_hidden()
    y_stage(0, 4)
    y_stage(0, 3)
    c_stage(0, 1)
    c_stage(0, 2)
    s_stage(2, 1)
    c_stage(0, 4)
    st_stage(4)
    normalise()
    c_stage(0, 3)
    s_stage(3, 0)
    w_ready(0)
    query_projection()
    attend([zslot(1), zslot(5)])
    s_stage(3, 1)
    keyval_projection()
    attend_own()
    s_stage(4, 0)
    attend([zslot(3), zslot(7)])
    attend([zslot(2), zslot(6)])
    s_stage(4, 1)
    finish_attention(zslot(4))
    output_projection()

    for copy in sends:
        copy.wait_send()

    @pl.when(c == h)
    def _():
        for ph in range(len(PHASES)):
            for copy in w_first_copies(ph):
                copy.wait_send()


def body(latents, timestep, gn_gain, gn_shift, temb_weight, w_query, w_keyval, w_out, stale_kv):
    vmem = pl.BlockSpec(memory_space=pltpu.VMEM)
    hbm = pl.BlockSpec(memory_space=pl.ANY)
    dma = pltpu.SemaphoreType.DMA
    phases = len(PHASES)
    scratch = [
        pltpu.VMEM((TOK, D), BF),
        pltpu.VMEM((1, D), F32),
        pltpu.VMEM((1, D), F32),
        pltpu.VMEM((TEMB, D), BF),
        pltpu.VMEM((80, 4 * D), BF),
        pltpu.VMEM((5, 80, 128), BF),
        pltpu.VMEM((5, NY, D, 128), BF),
        pltpu.VMEM((NZ, 2, 2, TOK, HALF), BF),
        pltpu.VMEM((2, TOK, D), BF),
        pltpu.VMEM((2 * TOK, D), F32),
        pltpu.VMEM((2 * TOK, D), BF),
        pltpu.VMEM((D, 128), BF),
        pltpu.VMEM((8, 128), F32),
        pltpu.VMEM((NZ, 2, 8, 128), F32),
        pltpu.VMEM((5, 256, 128), BF),
        pltpu.VMEM((5, 128, 128), BF),
        pltpu.VMEM((5, 128, 128), BF),
        pltpu.VMEM((5, 1, 256), F32),
        pltpu.VMEM((5, 1, 256), F32),
        pltpu.VMEM((5, 64, 256), F32),
        pltpu.VMEM((2 * TOK, D), BF),
        pltpu.VMEM((5, TOK, 128), BF),
        pltpu.VMEM((5, TOK, 128), BF),
        dma((7,)),
        dma((phases, 3)), dma((phases,)),
        dma((phases, 7)), dma((phases, 7)),
        dma((phases, 8, 3)), dma((phases, 8, 3)),
        dma((phases, 8)), dma((phases, 8)),
        dma, dma,
        dma, dma,
        dma((7, 2)), dma((7, 2)),
        dma,
        dma, dma,
        dma((7,)), dma((7,)),
        dma((5,)), dma((5,)),
        dma((5,)), dma((5,)),
    ]
    return pl.pallas_call(
        kernel,
        out_shape=jax.ShapeDtypeStruct((TOK, D), BF),
        in_specs=[pl.BlockSpec(memory_space=pltpu.SMEM)] + [hbm] * 8,
        out_specs=vmem,
        scratch_shapes=scratch,
        compiler_params=pltpu.CompilerParams(
            collective_id=0, has_side_effects=True, vmem_limit_bytes=60 * 1024 * 1024
        ),
        name="midblock_attention",
    )(
        timestep, latents, gn_gain, gn_shift, temb_weight,
        w_query, w_keyval, w_out, stale_kv,
    )


def solution(mesh):
    in_specs = (
        P(("img", "patch"), None),
        P("img"),
        P(),
        P(),
        P(),
        P("patch", None),
        P("patch", None),
        P("patch", None),
        P(None, ("img", "patch"), None),
    )
    out_specs = P(("img", "patch"), None)
    return jax.shard_map(body, mesh=mesh, in_specs=in_specs, out_specs=out_specs, check_vma=False)
```
